32 devices in a mesh: section: 2 (over x), peer: 16 (over z, y, core).
Axes of the slice: x: 2, y: 2, z: 4, core: 2. Of those that a mesh axis runs over, the one named last changes fastest.
Arguments:
- saved_inputs: bfloat16 [2, 16, 16, 8, 7168], P('section', 'peer'), may hold values from -6 to 6
- incoming: bfloat16 [2, 16, 16, 8, 7168], P('section', 'peer'), may hold values from -6 to 6
- norm_gain: bfloat16 [2, 16, 7168], P('section', 'peer'), may hold values from 0.5 to 1.5
- adapter: bfloat16 [2, 16, 2, 64, 7168], P('section', 'peer'), as said below
- wiring: int32 [2, 16, 16], replicated, may hold values from 0 to 15, as said below
- counts: int32 [2, 16], replicated, may hold values from 1 to 16, as said below
Outputs:
- routed_grads: bfloat16 [2, 16, 16, 8, 7168], P('section', 'peer')
- new_adapter: bfloat16 [2, 16, 2, 64, 7168], P('section', 'peer')
The draws below stay inside these ranges and needn't reach their ends.
Inputs may be any that keep to these rules, and one draw needn't show every extreme that they name: For s >= 1, slot j of peer p of section s goes to peer wiring[s, p, j] of section s - 1; section 0's entries are not read. Each peer's 16 slots name 16 different peers, and each peer is named 16 times a section. Over active slots no peer receives more than 16 micro-batches and no peer sends more than 1 to one peer; in every section some peer receives exactly 16. `counts`: in every section 8 or more peers have 16. `adapter`: entries of index 0 have a spread of 1/sqrt(7168), those of index 1 of 1/sqrt(64).
All inputs are finite; a program needn't handle non-finite values.
Results may differ from the reference program's by a relative error of at most 0.005.
Values may be sent and summed in bfloat16 or wider, within the bound.
No kernel may reach another device: no remote copies, remote signals or barrier semaphores. Data moves between devices by JAX's collectives and lax.ppermute only.
A program may use at most 64 MiB of HBM per device.

```python
import jax
import jax.numpy as jnp
from jax import lax

D = 7168
R = 64
MB = 8
CAP = 16
SECTIONS = 2
PEERS = 16


def routing_tables(key):
    section_keys = jax.random.split(key, SECTIONS)

    def one_section(section_key):
        several = jax.random.split(section_key, 6)
        shuffle = jax.random.permutation(several[0], PEERS)
        relabel = jax.random.permutation(several[1], PEERS)
        offsets = jax.random.permutation(several[2], PEERS)[:CAP]
        order = jax.random.permutation(several[3], CAP)
        slot_offset = offsets[order]
        wires = relabel[(shuffle[:, None] + slot_offset[None, :]) % PEERS]
        full_peer = jax.random.randint(several[4], (), 0, PEERS)
        chosen = jnp.any(wires == full_peer, axis=1)
        spread = jax.random.randint(several[5], (PEERS,), 1, CAP + 1)
        loads = jnp.where(chosen, CAP, spread)
        return (wires.astype(jnp.int32), loads.astype(jnp.int32))
    return jax.vmap(one_section)(section_keys)


def draw_wiring(key, part):
    tables = routing_tables(key)
    return tables[0]


def draw_counts(key, part):
    tables = routing_tables(key)
    return tables[1]


def draw_adapter(key, part):
    key = jax.random.fold_in(key, 11)
    shape = (SECTIONS, PEERS, 2, R, D)
    scales = jnp.array([D ** (-0.5), R ** (-0.5)], jnp.float32)[:, None, None]
    base = jax.random.normal(key, shape, jnp.float32)
    return (base * scales).astype(jnp.bfloat16)


def level_of(key, shape, cuts, smallest, largest):
    def one(dim, parts):
        draws = jax.random.uniform(jax.random.fold_in(jax.random.fold_in(key, 6), dim), (parts,), jnp.float32, smallest / len(cuts), largest / len(cuts))
        return jnp.repeat(jnp.exp(draws), shape[dim] // parts).reshape((-1,) + (1,) * (len(shape) - dim - 1))

    loudness = one(*cuts[0])
    for cut in cuts[1:]:
        loudness = loudness * one(*cut)
    return loudness


def gaussian(rng, shape, deviation, most, shards=(), kind=jnp.bfloat16):
    result = deviation * jax.random.normal(rng, shape, jnp.float32)
    if shards:
        result = result * level_of(rng, shape, shards, -0.22, 0.18)
    return jnp.clip(result, -most, most).astype(kind)


def setup_inputs(seed: int = 0) -> dict:
    streams_of = jax.random.split(jax.random.key(seed), 7)
    return {
        "saved_inputs": gaussian(streams_of[0], (SECTIONS, PEERS, CAP, MB, D), 1.0, 6.0, ((0, 2), (1, 16))),
        "incoming": gaussian(streams_of[1], (SECTIONS, PEERS, CAP, MB, D), 1.0, 6.0, ((0, 2), (1, 16))),
        "norm_gain": jnp.clip(1.0 + 0.1 * jax.random.normal(streams_of[2], (SECTIONS, PEERS, D), jnp.float32), 0.5, 1.5).astype(jnp.bfloat16),
        "adapter": draw_adapter(jax.random.fold_in(streams_of[6], 71), 0),
        "wiring": draw_wiring(jax.random.fold_in(streams_of[6], 71), 0),
        "counts": draw_counts(jax.random.fold_in(streams_of[6], 71), 0),
    }


norm_eps = 1e-05
rate_down = 5e-05
rate_up = 0.003
inner_dims = (((1,), (1,)), ((), ()))
outer_dims = (((0,), (0,)), ((), ()))

def block_backward(saved_block, incoming_block, gain_row, adapter_block, active_slots):
    slot_count, rows_each, features = saved_block.shape
    total_rows = slot_count * rows_each
    row_active = jnp.repeat(active_slots, rows_each).astype(incoming_block.dtype)[:, None]
    upstream = incoming_block.reshape(total_rows, features) * row_active
    inputs_full = saved_block.reshape(total_rows, features).astype(jnp.float32)
    centred = inputs_full - lax.optimization_barrier(jnp.mean(inputs_full, axis=1, keepdims=True))
    inv_scale = lax.rsqrt(lax.optimization_barrier(jnp.mean(centred * centred, axis=1, keepdims=True)) + norm_eps)
    unit_rows = centred * inv_scale
    gain_full = gain_row.astype(jnp.float32)[None, :]
    normed = (unit_rows * gain_full).astype(jnp.bfloat16)
    down_proj = adapter_block[0]
    up_proj = adapter_block[1]
    pre_act = lax.dot_general(normed, down_proj, inner_dims, preferred_element_type=jnp.float32)
    act_value, act_pull = jax.vjp(jax.nn.gelu, pre_act)
    hidden = act_value.astype(jnp.bfloat16)
    grad_up = lax.dot_general(hidden, upstream, outer_dims, preferred_element_type=jnp.float32)
    grad_hidden = lax.dot_general(upstream, up_proj, inner_dims, preferred_element_type=jnp.float32)
    grad_pre = act_pull(grad_hidden)[0].astype(jnp.bfloat16)
    grad_down = lax.dot_general(grad_pre, normed, outer_dims, preferred_element_type=jnp.float32)
    grad_normed = jnp.dot(grad_pre, down_proj, preferred_element_type=jnp.float32)
    scaled = grad_normed * gain_full
    grad_input = upstream.astype(jnp.float32) + inv_scale * (scaled - lax.optimization_barrier(jnp.mean(scaled, axis=1, keepdims=True)) - unit_rows * lax.optimization_barrier(jnp.mean(scaled * unit_rows, axis=1, keepdims=True)))
    new_down = (down_proj.astype(jnp.float32) - rate_down * grad_down).astype(jnp.bfloat16)
    new_up = (up_proj.astype(jnp.float32) - rate_up * grad_up).astype(jnp.bfloat16)
    return (grad_input.astype(jnp.bfloat16).reshape(slot_count, rows_each, features), new_down, new_up)

def reference(saved_inputs, incoming, norm_gain, adapter, wiring, counts):
    slot_ids = jnp.arange(CAP, dtype=jnp.int32)
    active = slot_ids[None, None, :] < counts[:, :, None]

    def per_device(packed):
        return block_backward(packed[0], packed[1], packed[2], packed[3], packed[4])

    def flatten(values_in):
        return values_in.reshape((SECTIONS * PEERS,) + values_in.shape[2:])
    grad_input, new_down, new_up = lax.map(per_device, (flatten(saved_inputs), flatten(incoming), flatten(norm_gain), flatten(adapter), flatten(active)))
    stepped = jnp.stack([new_down, new_up], axis=1).reshape(SECTIONS, PEERS, 2, R, D).astype(jnp.float32)
    new_adapter = ((jnp.roll(stepped, 1, axis=1) + stepped + jnp.roll(stepped, -1, axis=1)) / 3.0).astype(jnp.bfloat16)
    grad_input = grad_input.reshape(SECTIONS, PEERS * CAP, MB, D)
    peer_ids = jnp.arange(PEERS, dtype=jnp.int32)
    routed = []
    for section_id in range(1, SECTIONS):
        targets = wiring[section_id].reshape(-1)
        slot_flags = active[section_id].reshape(-1)
        onehot = ((targets[:, None] == peer_ids[None, :]) & slot_flags[:, None]).astype(jnp.int32)
        earlier = lax.optimization_barrier(jnp.sum((jnp.cumsum(onehot, axis=0) - onehot) * onehot, axis=1))
        destination = jnp.where(slot_flags, targets * CAP + earlier, PEERS * CAP).astype(jnp.int32)
        holder = jnp.zeros((PEERS * CAP + 1, MB, D), jnp.bfloat16).at[destination].set(grad_input[section_id])
        routed.append(holder[:PEERS * CAP])
    routed.append(jnp.zeros((PEERS * CAP, MB, D), jnp.bfloat16))
    routed_grads = jnp.stack(routed).reshape(SECTIONS, PEERS, CAP, MB, D)
    return (routed_grads, new_adapter)
```

```python
import functools

import jax
import jax.numpy as jnp
from jax import lax
from jax.experimental import pallas as pl
from jax.experimental.pallas import tpu as pltpu
from jax.sharding import PartitionSpec as P

norm_eps = 1e-05
rate_down = 5e-05
rate_up = 0.003
inner_dims = (((1,), (1,)), ((), ()))
outer_dims = (((0,), (0,)), ((), ()))
AXES = ("section", "peer")
TILE = 1024
F32 = jnp.float32
BF16 = jnp.bfloat16


def column_tile(features):
    return TILE if features % TILE == 0 else 128


def split_peer(peer):
    return peer // 4, (peer // 2) % 2, peer % 2


def step_kernel(outer_total, wiring_ref, counts_ref, x_hbm, g_hbm, gain_ref, adapter_hbm, *rest):
    trips = 2 * outer_total
    grads_out = rest[:trips]
    down_out, up_out = rest[trips : trips + 2]
    x, g, adapter, normed, upstream, grads, steps, mean_s, inv_s, x_sem, in_sem, out_sem = rest[trips + 2 :]
    slots, rows_each, features = x.shape
    rows = slots * rows_each
    section, peer = lax.axis_index("section"), lax.axis_index("peer")
    outer, side, core = split_peer(peer)
    parts = x_sem.shape[0]
    each = slots // parts
    tile = column_tile(features)

    x_copies = [
        pltpu.make_async_copy(x_hbm.at[pl.ds(i * each, each)], x.at[pl.ds(i * each, each)], x_sem.at[i])
        for i in range(parts)
    ]
    for copy in x_copies:
        copy.start()
    adapter_copy = pltpu.make_async_copy(adapter_hbm, adapter, in_sem.at[0])
    adapter_copy.start()
    g_copy = pltpu.make_async_copy(g_hbm, g, in_sem.at[1])
    g_copy.start()

    def stats(slot):
        block = x[slot].astype(F32)
        mean = jnp.mean(block, axis=1, keepdims=True)
        centred = block - mean
        var = jnp.mean(centred * centred, axis=1, keepdims=True)
        row = pl.ds(pl.multiple_of(slot * rows_each, rows_each), rows_each)
        mean_s[row, :] = jnp.broadcast_to(mean, (rows_each, 128))
        inv_s[row, :] = jnp.broadcast_to(lax.rsqrt(var + norm_eps), (rows_each, 128))

    for i in range(parts):
        x_copies[i].wait()
        for j in range(each):
            stats(i * each + j)

    mean = mean_s[:, :1]
    inv = inv_s[:, :1]
    live = lax.broadcasted_iota(jnp.int32, (rows, 1), 0) < counts_ref[section, peer] * rows_each

    adapter_copy.wait()
    g_copy.wait()

    def first(i, carry):
        pre, pulled, gained = carry
        cols = pl.ds(pl.multiple_of(i * tile, tile), tile)
        unit = (x[:, :, cols].astype(F32).reshape(rows, tile) - mean) * inv
        gain = gain_ref[:, cols].astype(F32)
        scaled = (unit * gain).astype(BF16)
        normed[:, cols] = scaled
        ups = jnp.where(live, g[:, :, cols].astype(F32).reshape(rows, tile), 0.0).astype(BF16)
        upstream[:, cols] = ups
        down = adapter[0, :, cols]
        pre = pre + lax.dot_general(scaled, down, inner_dims, preferred_element_type=F32)
        pulled = pulled + lax.dot_general(ups, adapter[1, :, cols], inner_dims, preferred_element_type=F32)
        gains = jnp.broadcast_to(gain_ref[:, cols], (16, tile))
        gained = gained + lax.dot_general(gains, down, inner_dims, preferred_element_type=F32)
        return pre, pulled, gained

    hidden_units = adapter.shape[1]
    zero = jnp.zeros((rows, hidden_units), F32)
    pre_act, grad_hidden, gained = lax.fori_loop(
        0, features // tile, first, (zero, zero, jnp.zeros((16, hidden_units), F32)), unroll=True
    )
    act_value, act_pull = jax.vjp(jax.nn.gelu, pre_act)
    hidden = act_value.astype(BF16)
    grad_pre = act_pull(grad_hidden)[0].astype(BF16)
    grad_pre_full = grad_pre.astype(F32)
    mean_v = jnp.sum(grad_pre_full * gained[:1], axis=1, keepdims=True) / features
    mean_vu = jnp.sum(grad_pre_full * pre_act, axis=1, keepdims=True) / features

    targets = []
    for j in range(slots):
        outer_to, side_to, core_to = split_peer(wiring_ref[section, peer, j])
        hop = lax.rem(outer_to - outer + outer_total, outer_total)
        targets.append((hop * 2 + (side_to + side) % 2) * 2 + (core_to + core) % 2)

    def second(i, carry):
        cols = pl.ds(pl.multiple_of(i * tile, tile), tile)
        down = adapter[0, :, cols]
        gain = gain_ref[:, cols].astype(F32)
        unit = (x[:, :, cols].astype(F32).reshape(rows, tile) - mean) * inv
        scaled = jnp.dot(grad_pre, down, preferred_element_type=F32) * gain
        ups = upstream[:, cols]
        result = ups.astype(F32) + inv * (scaled - mean_v - unit * mean_vu)
        result = result.reshape(slots, rows_each, tile).astype(BF16)
        for j in range(slots):
            grads[targets[j], :, cols] = result[j]
        grad_down = lax.dot_general(grad_pre, normed[:, cols], outer_dims, preferred_element_type=F32)
        grad_up = lax.dot_general(hidden, ups, outer_dims, preferred_element_type=F32)
        steps[0, :, cols] = (down.astype(F32) - rate_down * grad_down).astype(BF16)
        steps[1, :, cols] = (adapter[1, :, cols].astype(F32) - rate_up * grad_up).astype(BF16)
        return carry

    lax.fori_loop(0, features // tile, second, 0, unroll=True)
    copies = [
        pltpu.make_async_copy(steps.at[0], down_out, out_sem.at[trips]),
        pltpu.make_async_copy(steps.at[1], up_out, out_sem.at[trips + 1]),
    ]
    for k in range(trips):
        copies.append(pltpu.make_async_copy(grads.at[pl.ds(2 * k, 2)], grads_out[k], out_sem.at[k]))
    for copy in copies:
        copy.start()
    for copy in copies:
        copy.wait()


def step(outer_total, saved, incoming, gain, adapter, wiring, counts):
    slots, rows_each, features = saved.shape
    units = adapter.shape[1]
    rows = slots * rows_each
    trips = 2 * outer_total
    parts = 4 if slots % 4 == 0 else 1
    hbm = pl.BlockSpec(memory_space=pl.ANY)
    smem = pl.BlockSpec(memory_space=pltpu.SMEM)
    vmem = pl.BlockSpec(memory_space=pltpu.VMEM)
    results = pl.pallas_call(
        functools.partial(step_kernel, outer_total),
        out_shape=[jax.ShapeDtypeStruct((2, rows_each, features), BF16)] * trips
        + [jax.ShapeDtypeStruct((units, features), BF16)] * 2,
        in_specs=[smem, smem, hbm, hbm, vmem, hbm],
        out_specs=[hbm] * (trips + 2),
        scratch_shapes=[
            pltpu.VMEM((slots, rows_each, features), BF16),
            pltpu.VMEM((slots, rows_each, features), BF16),
            pltpu.VMEM((2, units, features), BF16),
            pltpu.VMEM((rows, features), BF16),
            pltpu.VMEM((rows, features), BF16),
            pltpu.VMEM((2 * trips, rows_each, features), BF16),
            pltpu.VMEM((2, units, features), BF16),
            pltpu.VMEM((rows, 128), F32),
            pltpu.VMEM((rows, 128), F32),
            pltpu.SemaphoreType.DMA((parts,)),
            pltpu.SemaphoreType.DMA((2,)),
            pltpu.SemaphoreType.DMA((trips + 2,)),
        ],
        compiler_params=pltpu.CompilerParams(vmem_limit_bytes=40 * 1024 * 1024),
        cost_estimate=pl.CostEstimate(
            flops=10 * rows * units * features, bytes_accessed=10 * rows * features, transcendentals=0
        ),
    )(wiring, counts, saved, incoming, gain, adapter)
    return results[:trips], results[trips], results[trips + 1]


def place_kernel(outer_total, places_ref, *rest):
    trips = 2 * outer_total
    kept = rest[:trips]
    crossed, out, blank, sem = rest[trips:]
    slots = out.shape[0]
    outer, side, core = split_peer(lax.axis_index("peer"))
    arrived = places_ref[4 * outer_total]
    blank[...] = jnp.zeros_like(blank)
    pairs = []
    for k in range(trips):
        source_outer = lax.rem(outer - k // 2 + outer_total, outer_total)
        source = source_outer * 4 + (side + k % 2) % 2 * 2
        pairs.append((places_ref[source + core], kept[k].at[0], k))
        pairs.append((places_ref[source + 1 - core], crossed.at[k], trips + k))

    def put(place, block, index):
        return pltpu.make_async_copy(block, out.at[jnp.clip(place, 0, slots - 1)], sem.at[index])

    for place, block, index in pairs:
        pl.when(place >= 0)(lambda place=place, block=block, index=index: put(place, block, index).start())
    for j in range(slots):
        pl.when(j >= arrived)(lambda j=j: put(j, blank, 2 * trips + j).start())
    for place, block, index in pairs:
        pl.when(place >= 0)(lambda place=place, block=block, index=index: put(place, block, index).wait())
    for j in range(slots):
        pl.when(j >= arrived)(lambda j=j: put(j, blank, 2 * trips + j).wait())


def place(outer_total, places, kept, crossed, slots):
    trips = 2 * outer_total
    hbm = pl.BlockSpec(memory_space=pl.ANY)
    _, rows_each, features = crossed.shape
    return pl.pallas_call(
        functools.partial(place_kernel, outer_total),
        out_shape=jax.ShapeDtypeStruct((slots, rows_each, features), BF16),
        in_specs=[pl.BlockSpec(memory_space=pltpu.SMEM)] + [hbm] * (trips + 1),
        out_specs=hbm,
        scratch_shapes=[
            pltpu.VMEM((rows_each, features), BF16),
            pltpu.SemaphoreType.DMA((2 * trips + slots,)),
        ],
        cost_estimate=pl.CostEstimate(
            flops=0, bytes_accessed=4 * slots * rows_each * features, transcendentals=0
        ),
    )(places, *kept, crossed)


def arrival_places(section, peer, section_total, wiring, counts):
    sender_section = jnp.minimum(section + 1, section_total - 1)
    slot_ids = jnp.arange(wiring.shape[2], dtype=jnp.int32)
    active = slot_ids[None, :] < counts[sender_section][:, None]
    sends = jnp.any((wiring[sender_section] == peer) & active, axis=1) & (section + 1 < section_total)
    sends = sends.astype(jnp.int32)
    ids = jnp.arange(sends.shape[0], dtype=jnp.int32)
    earlier = jnp.sum(jnp.where(ids[None, :] < ids[:, None], sends[None, :], 0), axis=1)
    places = jnp.where(sends > 0, earlier, -1)
    return jnp.concatenate([places, jnp.sum(sends)[None]])


def peer_index(outer, side, core):
    return outer * 4 + side * 2 + core


def trip_pairs(section_total, outer_total, hop, cross):
    peers = 4 * outer_total
    pairs = []
    for section in range(1, section_total):
        for outer in range(outer_total):
            for side in range(2):
                for core in range(2):
                    source = section * peers + peer_index(outer, side, core)
                    target = peer_index((outer + hop) % outer_total, side ^ cross, core)
                    pairs.append((source, (section - 1) * peers + target))
    return pairs


def around(value, steps):
    count = lax.axis_size("peer")
    return lax.ppermute(value, "peer", [(p, (p + steps) % count) for p in range(count)])


def three_mean(left_part, centre_part, right_part):
    total = left_part.astype(F32) + centre_part.astype(F32) + right_part.astype(F32)
    return (total / 3.0).astype(BF16)


def per_device(saved_inputs, incoming, norm_gain, adapter, wiring, counts):
    peer_total = lax.axis_size("peer")
    section_total = lax.axis_size("section")
    outer_total = peer_total // 4
    section, peer = lax.axis_index("section"), lax.axis_index("peer")
    slots = saved_inputs.shape[2]
    blocks, new_down, new_up = step(
        outer_total, saved_inputs[0, 0], incoming[0, 0], norm_gain[0], adapter[0, 0], wiring, counts
    )
    places = arrival_places(section, peer, section_total, wiring, counts)
    arrived = []
    for k in range(2 * outer_total):
        pairs = trip_pairs(section_total, outer_total, k // 2, k % 2)
        arrived.append(lax.ppermute(blocks[k], AXES, pairs))
    stepped = [new_down, new_up]
    lefts = [around(part, 1) for part in stepped]
    rights = [around(part, -1) for part in stepped]
    crossing = jnp.stack([part[1] for part in arrived])
    crossed = lax.ppermute(crossing, "peer", [(p, p ^ 1) for p in range(peer_total)])
    routed = place(outer_total, places, arrived, crossed, slots)
    averaged = jnp.stack([three_mean(*parts) for parts in zip(lefts, stepped, rights)])
    return (routed[None, None], averaged[None, None])


def solution(mesh):
    return jax.shard_map(
        per_device,
        mesh=mesh,
        in_specs=(
            P("section", "peer", None, None, None),
            P("section", "peer", None, None, None),
            P("section", "peer", None),
            P("section", "peer", None, None, None),
            P(),
            P(),
        ),
        out_specs=(P("section", "peer", None, None, None), P("section", "peer", None, None, None)),
        check_vma=False,
    )
```

```python
import functools

import jax
import jax.numpy as jnp
from jax import lax
from jax.experimental import pallas as pl
from jax.experimental.pallas import tpu as pltpu
from jax.sharding import PartitionSpec as P

norm_eps = 1e-05
rate_down = 5e-05
rate_up = 0.003
inner_dims = (((1,), (1,)), ((), ()))
outer_dims = (((0,), (0,)), ((), ()))
AXES = ("section", "peer")
TILE = 1024
VMEM_BYTES = 60 * 1024 * 1024
F32 = jnp.float32
BF16 = jnp.bfloat16


def column_tile(features):
    return TILE if features % TILE == 0 else 128


def split_peer(peer):
    return peer // 4, (peer // 2) % 2, peer % 2


def step_kernel(outer_total, wiring_hbm, counts_hbm, x_hbm, g_hbm, gain_hbm, adapter_hbm, *rest):
    trips = 2 * outer_total
    grads_out = rest[:trips]
    steps_out = rest[trips]
    (wiring_ref, counts_ref, gain_ref, x, g, adapter, normed, upstream, grads, steps, mean_s, inv_s) = rest[
        trips + 1 : trips + 13
    ]
    x_sem, in_sem, out_sem = rest[trips + 13 :]
    slots, rows_each, features = x.shape
    rows = slots * rows_each
    section, peer = lax.axis_index("section"), lax.axis_index("peer")
    outer, side, core = split_peer(peer)
    parts = x_sem.shape[0]
    each = slots // parts
    tile = column_tile(features)

    x_copies = [
        pltpu.make_async_copy(x_hbm.at[pl.ds(i * each, each)], x.at[pl.ds(i * each, each)], x_sem.at[i])
        for i in range(parts)
    ]
    for copy in x_copies:
        copy.start()
    small_copies = [
        pltpu.make_async_copy(source, target, in_sem.at[2 + i])
        for i, (source, target) in enumerate(
            ((wiring_hbm, wiring_ref), (counts_hbm, counts_ref), (gain_hbm, gain_ref))
        )
    ]
    for copy in small_copies:
        copy.start()
    adapter_copy = pltpu.make_async_copy(adapter_hbm, adapter, in_sem.at[0])
    adapter_copy.start()
    g_copy = pltpu.make_async_copy(g_hbm, g, in_sem.at[1])
    g_copy.start()

    def stats(slot):
        block = x[slot].astype(F32)
        mean = jnp.mean(block, axis=1, keepdims=True)
        centred = block - mean
        var = jnp.mean(centred * centred, axis=1, keepdims=True)
        row = pl.ds(pl.multiple_of(slot * rows_each, rows_each), rows_each)
        mean_s[row, :] = jnp.broadcast_to(mean, (rows_each, 128))
        inv_s[row, :] = jnp.broadcast_to(lax.rsqrt(var + norm_eps), (rows_each, 128))

    for i in range(parts):
        x_copies[i].wait()
        for j in range(each):
            stats(i * each + j)

    for copy in small_copies:
        copy.wait()
    mean = mean_s[:, :1]
    inv = inv_s[:, :1]
    live = lax.broadcasted_iota(jnp.int32, (rows, 1), 0) < counts_ref[section, peer] * rows_each

    adapter_copy.wait()
    g_copy.wait()

    def first(i, carry):
        pre, pulled, gained = carry
        cols = pl.ds(pl.multiple_of(i * tile, tile), tile)
        unit = (x[:, :, cols].astype(F32).reshape(rows, tile) - mean) * inv
        gain = gain_ref[:, cols].astype(F32)
        scaled = (unit * gain).astype(BF16)
        normed[:, cols] = scaled
        ups = jnp.where(live, g[:, :, cols].astype(F32).reshape(rows, tile), 0.0).astype(BF16)
        upstream[:, cols] = ups
        down = adapter[0, :, cols]
        pre = pre + lax.dot_general(scaled, down, inner_dims, preferred_element_type=F32)
        pulled = pulled + lax.dot_general(ups, adapter[1, :, cols], inner_dims, preferred_element_type=F32)
        gains = jnp.broadcast_to(gain_ref[:, cols], (16, tile))
        gained = gained + lax.dot_general(gains, down, inner_dims, preferred_element_type=F32)
        return pre, pulled, gained

    hidden_units = adapter.shape[1]
    zero = jnp.zeros((rows, hidden_units), F32)
    pre_act, grad_hidden, gained = lax.fori_loop(
        0, features // tile, first, (zero, zero, jnp.zeros((16, hidden_units), F32)), unroll=True
    )
    act_value, act_pull = jax.vjp(jax.nn.gelu, pre_act)
    hidden = act_value.astype(BF16)
    grad_pre = act_pull(grad_hidden)[0].astype(BF16)
    grad_pre_full = grad_pre.astype(F32)
    mean_v = jnp.sum(grad_pre_full * gained[:1], axis=1, keepdims=True) / features
    mean_vu = jnp.sum(grad_pre_full * pre_act, axis=1, keepdims=True) / features

    targets = []
    for j in range(slots):
        outer_to, side_to, core_to = split_peer(wiring_ref[section, peer, j])
        hop = lax.rem(outer_to - outer + outer_total, outer_total)
        targets.append((hop * 2 + (side_to + side) % 2) * 2 + (core_to + core) % 2)

    def second(i, carry):
        cols = pl.ds(pl.multiple_of(i * tile, tile), tile)
        down = adapter[0, :, cols]
        gain = gain_ref[:, cols].astype(F32)
        unit = (x[:, :, cols].astype(F32).reshape(rows, tile) - mean) * inv
        scaled = jnp.dot(grad_pre, down, preferred_element_type=F32) * gain
        ups = upstream[:, cols]
        result = ups.astype(F32) + inv * (scaled - mean_v - unit * mean_vu)
        result = result.reshape(slots, rows_each, tile).astype(BF16)
        for j in range(slots):
            grads[targets[j], :, cols] = result[j]
        grad_down = lax.dot_general(grad_pre, normed[:, cols], outer_dims, preferred_element_type=F32)
        grad_up = lax.dot_general(hidden, ups, outer_dims, preferred_element_type=F32)
        steps[0, :, cols] = (down.astype(F32) - rate_down * grad_down).astype(BF16)
        steps[1, :, cols] = (adapter[1, :, cols].astype(F32) - rate_up * grad_up).astype(BF16)
        return carry

    lax.fori_loop(0, features // tile, second, 0, unroll=True)
    copies = [
        pltpu.make_async_copy(steps, steps_out, out_sem.at[trips]),
    ]
    for k in range(trips):
        copies.append(pltpu.make_async_copy(grads.at[pl.ds(2 * k, 2)], grads_out[k], out_sem.at[k]))
    for copy in copies:
        copy.start()
    for copy in copies:
        copy.wait()


def step(outer_total, saved, incoming, gain, adapter, wiring, counts):
    slots, rows_each, features = saved.shape
    units = adapter.shape[1]
    rows = slots * rows_each
    trips = 2 * outer_total
    parts = 4 if slots % 4 == 0 else 1
    hbm = pl.BlockSpec(memory_space=pl.ANY)
    results = pl.pallas_call(
        functools.partial(step_kernel, outer_total),
        out_shape=[jax.ShapeDtypeStruct((2, rows_each, features), BF16)] * trips
        + [jax.ShapeDtypeStruct((2, units, features), BF16)],
        in_specs=[hbm] * 6,
        out_specs=[hbm] * (trips + 1),
        scratch_shapes=[
            pltpu.SMEM(wiring.shape, jnp.int32),
            pltpu.SMEM(counts.shape, jnp.int32),
            pltpu.VMEM(gain.shape, BF16),
            pltpu.VMEM((slots, rows_each, features), BF16),
            pltpu.VMEM((slots, rows_each, features), BF16),
            pltpu.VMEM((2, units, features), BF16),
            pltpu.VMEM((rows, features), BF16),
            pltpu.VMEM((rows, features), BF16),
            pltpu.VMEM((2 * trips, rows_each, features), BF16),
            pltpu.VMEM((2, units, features), BF16),
            pltpu.VMEM((rows, 128), F32),
            pltpu.VMEM((rows, 128), F32),
            pltpu.SemaphoreType.DMA((parts,)),
            pltpu.SemaphoreType.DMA((5,)),
            pltpu.SemaphoreType.DMA((trips + 1,)),
        ],
        compiler_params=pltpu.CompilerParams(vmem_limit_bytes=VMEM_BYTES),
        cost_estimate=pl.CostEstimate(
            flops=10 * rows * units * features, bytes_accessed=10 * rows * features, transcendentals=0
        ),
    )(wiring, counts, saved, incoming, gain, adapter)
    return results[:trips], results[trips]


def place_kernel(outer_total, places_ref, *rest):
    trips = 2 * outer_total
    kept = rest[:trips]
    crossed, out, blank, sem = rest[trips:]
    slots = out.shape[0]
    outer, side, core = split_peer(lax.axis_index("peer"))
    arrived = places_ref[4 * outer_total]
    blank[...] = jnp.zeros_like(blank)
    pairs = []
    for k in range(trips):
        source_outer = lax.rem(outer - k // 2 + outer_total, outer_total)
        source = source_outer * 4 + (side + k % 2) % 2 * 2
        pairs.append((places_ref[source + core], kept[k].at[0], k))
        pairs.append((places_ref[source + 1 - core], crossed.at[k], trips + k))

    def put(place, block, index):
        return pltpu.make_async_copy(block, out.at[jnp.clip(place, 0, slots - 1)], sem.at[index])

    for place, block, index in pairs:
        pl.when(place >= 0)(lambda place=place, block=block, index=index: put(place, block, index).start())
    for j in range(slots):
        pl.when(j >= arrived)(lambda j=j: put(j, blank, 2 * trips + j).start())
    for place, block, index in pairs:
        pl.when(place >= 0)(lambda place=place, block=block, index=index: put(place, block, index).wait())
    for j in range(slots):
        pl.when(j >= arrived)(lambda j=j: put(j, blank, 2 * trips + j).wait())


def place(outer_total, places, kept, crossed, slots):
    trips = 2 * outer_total
    vmem = pl.BlockSpec(memory_space=pltpu.VMEM)
    _, rows_each, features = crossed.shape
    return pl.pallas_call(
        functools.partial(place_kernel, outer_total),
        out_shape=jax.ShapeDtypeStruct((slots, rows_each, features), BF16),
        in_specs=[pl.BlockSpec(memory_space=pltpu.SMEM)] + [vmem] * (trips + 1),
        out_specs=pl.BlockSpec(memory_space=pl.ANY),
        scratch_shapes=[
            pltpu.VMEM((rows_each, features), BF16),
            pltpu.SemaphoreType.DMA((2 * trips + slots,)),
        ],
        cost_estimate=pl.CostEstimate(
            flops=0, bytes_accessed=4 * slots * rows_each * features, transcendentals=0
        ),
    )(places, *kept, crossed)


def arrival_places(section, peer, section_total, wiring, counts):
    sender_section = jnp.minimum(section + 1, section_total - 1)
    slot_ids = jnp.arange(wiring.shape[2], dtype=jnp.int32)
    active = slot_ids[None, :] < counts[sender_section][:, None]
    sends = jnp.any((wiring[sender_section] == peer) & active, axis=1) & (section + 1 < section_total)
    sends = sends.astype(jnp.int32)
    ids = jnp.arange(sends.shape[0], dtype=jnp.int32)
    earlier = jnp.sum(jnp.where(ids[None, :] < ids[:, None], sends[None, :], 0), axis=1)
    places = jnp.where(sends > 0, earlier, -1)
    return jnp.concatenate([places, jnp.sum(sends)[None]])


def peer_index(outer, side, core):
    return outer * 4 + side * 2 + core


def trip_pairs(section_total, outer_total, hop, cross):
    peers = 4 * outer_total
    pairs = []
    for section in range(1, section_total):
        for outer in range(outer_total):
            for side in range(2):
                for core in range(2):
                    source = section * peers + peer_index(outer, side, core)
                    target = peer_index((outer + hop) % outer_total, side ^ cross, core)
                    pairs.append((source, (section - 1) * peers + target))
    return pairs


def mean_of_three(one, two, three):
    total = one.astype(F32) + two.astype(F32) + three.astype(F32)
    return (total / 3.0).astype(BF16)


def per_device(saved_inputs, incoming, norm_gain, adapter, wiring, counts):
    peer_total = lax.axis_size("peer")
    section_total = lax.axis_size("section")
    outer_total = peer_total // 4
    section, peer = lax.axis_index("section"), lax.axis_index("peer")
    slots = saved_inputs.shape[2]
    blocks, stepped = step(
        outer_total, saved_inputs[0, 0], incoming[0, 0], norm_gain[0], adapter[0, 0], wiring, counts
    )
    places = arrival_places(section, peer, section_total, wiring, counts)
    partner = [(p, p ^ 1) for p in range(peer_total)]
    beyond = [(p, (p + 2 * (p % 2) - 1) % peer_total) for p in range(peer_total)]
    arrived = []
    for k in range(2 * outer_total):
        pairs = trip_pairs(section_total, outer_total, k // 2, k % 2)
        arrived.append(lax.ppermute(blocks[k], AXES, pairs))
    near = lax.ppermute(stepped, "peer", partner)
    far = lax.ppermute(stepped, "peer", beyond)
    crossing = jnp.concatenate([part[1:] for part in arrived])
    crossed = lax.ppermute(crossing, "peer", partner)
    routed = place(outer_total, places, arrived, crossed, slots)
    averaged = mean_of_three(near, stepped, far)
    return (routed[None, None], averaged[None, None])


def solution(mesh):
    return jax.shard_map(
        per_device,
        mesh=mesh,
        in_specs=(
            P("section", "peer", None, None, None),
            P("section", "peer", None, None, None),
            P("section", "peer", None),
            P("section", "peer", None, None, None),
            P(),
            P(),
        ),
        out_specs=(P("section", "peer", None, None, None), P("section", "peer", None, None, None)),
        check_vma=False,
    )
```

```python
import functools

import jax
import jax.numpy as jnp
from jax import lax
from jax.experimental import pallas as pl
from jax.experimental.pallas import tpu as pltpu
from jax.sharding import PartitionSpec as P

norm_eps = 1e-05
rate_down = 5e-05
rate_up = 0.003
inner_dims = (((1,), (1,)), ((), ()))
AXES = ("section", "peer")
TILE = 1024
AHEAD = 4
BAND = 64
ORDER = ("near", "far", "lift", "d00", "d31", "d30", "z20", "d11", "z21", "d01", "d10")
VMEM_BYTES = 60 * 1024 * 1024
F32 = jnp.float32
BF16 = jnp.bfloat16


def column_tile(features):
    return TILE if features % TILE == 0 else 128


def split_peer(peer):
    return peer // 4, (peer // 2) % 2, peer % 2


def expand(outer_total):
    relayed = outer_total // 2
    hops = {"0": [0], "1": range(1, relayed), "2": [relayed], "3": range(relayed + 1, outer_total)}
    order = []
    for name in ORDER:
        if name in ("near", "far", "lift", "swap"):
            order.append((name, 0, 0))
        else:
            order += [(name[0], hop, int(name[2])) for hop in hops[name[1]]]
    return order


def load_ranges(outer_total):
    order = expand(outer_total)
    loads = {}
    for name, hop, cross in order:
        if name == "lift":
            loads["lift"] = [(h, c) for n, h, c in order if n == "z"]
        if name == "swap":
            loads["swap"] = [(h, c) for n, h, c in order if n == "r"]
        if name == "d":
            loads[hop, cross] = [(hop, cross)]
    return loads


def step_kernel(outer_total, wiring_hbm, counts_hbm, x_hbm, g_hbm, gain_hbm, adapter_hbm, *rest):
    loads = load_ranges(outer_total)
    trips, count = 2 * outer_total, len(loads)
    grads_out = rest[:count]
    steps_out = rest[count]
    (wiring_ref, counts_ref, gain_ref, x, g, adapter, normed, upstream, grads, steps, mean_s, inv_s) = rest[
        count + 1 : count + 13
    ]
    x_sem, in_sem, out_sem = rest[count + 13 :]
    slots, rows_each, features = x.shape
    rows = slots * rows_each
    section, peer = lax.axis_index("section"), lax.axis_index("peer")
    outer, side, core = split_peer(peer)
    parts = x_sem.shape[0]
    each = slots // parts
    tile = column_tile(features)

    x_copies = [
        pltpu.make_async_copy(x_hbm.at[pl.ds(i * each, each)], x.at[pl.ds(i * each, each)], x_sem.at[i])
        for i in range(parts)
    ]
    for copy in x_copies:
        copy.start()
    small_copies = [
        pltpu.make_async_copy(source, target, in_sem.at[2 + i])
        for i, (source, target) in enumerate(
            ((wiring_hbm, wiring_ref), (counts_hbm, counts_ref), (gain_hbm, gain_ref))
        )
    ]
    for copy in small_copies:
        copy.start()
    adapter_copy = pltpu.make_async_copy(adapter_hbm, adapter, in_sem.at[0])
    adapter_copy.start()
    g_copy = pltpu.make_async_copy(g_hbm, g, in_sem.at[1])
    g_copy.start()

    def stats(slot):
        block = x[slot].astype(F32)
        mean = jnp.mean(block, axis=1, keepdims=True)
        centred = block - mean
        var = jnp.mean(centred * centred, axis=1, keepdims=True)
        row = pl.ds(pl.multiple_of(slot * rows_each, rows_each), rows_each)
        mean_s[row, :] = jnp.broadcast_to(mean, (rows_each, 128))
        inv_s[row, :] = jnp.broadcast_to(lax.rsqrt(var + norm_eps), (rows_each, 128))

    for i in range(parts):
        x_copies[i].wait()
        for j in range(each):
            stats(i * each + j)

    for copy in small_copies:
        copy.wait()
    mean = mean_s[:, :1]
    inv = inv_s[:, :1]
    live = lax.broadcasted_iota(jnp.int32, (rows, 1), 0) < counts_ref[section, peer] * rows_each

    adapter_copy.wait()
    g_copy.wait()

    def first(i, carry):
        pre, pulled, gained = carry
        cols = pl.ds(pl.multiple_of(i * tile, tile), tile)
        unit = (x[:, :, cols].astype(F32).reshape(rows, tile) - mean) * inv
        gain = gain_ref[:, cols].astype(F32)
        scaled = (unit * gain).astype(BF16)
        normed[:, cols] = scaled
        ups = jnp.where(live, g[:, :, cols].astype(F32).reshape(rows, tile), 0.0).astype(BF16)
        upstream[:, cols] = ups
        down = adapter[0, :, cols]
        pre = pre + lax.dot_general(scaled, down, inner_dims, preferred_element_type=F32)
        pulled = pulled + lax.dot_general(ups, adapter[1, :, cols], inner_dims, preferred_element_type=F32)
        gains = jnp.broadcast_to(gain_ref[:, cols], (16, tile))
        gained = gained + lax.dot_general(gains, down, inner_dims, preferred_element_type=F32)
        return pre, pulled, gained

    hidden_units = adapter.shape[1]
    zero = jnp.zeros((rows, hidden_units), F32)
    pre_act, grad_hidden, gained = lax.fori_loop(
        0, features // tile, first, (zero, zero, jnp.zeros((16, hidden_units), F32)), unroll=True
    )
    act_value, act_pull = jax.vjp(jax.nn.gelu, pre_act)
    grad_pre = act_pull(grad_hidden)[0].astype(BF16)
    grad_pre_full = grad_pre.astype(F32)
    mean_v = jnp.sum(grad_pre_full * gained[:1], axis=1, keepdims=True) / features
    mean_vu = jnp.sum(grad_pre_full * pre_act, axis=1, keepdims=True) / features

    targets = []
    for j in range(slots):
        outer_to, side_to, core_to = split_peer(wiring_ref[section, peer, j])
        hop = lax.rem(outer_to - outer + outer_total, outer_total)
        targets.append((hop * 2 + (side_to + side) % 2) * 2 + (core_to + core) % 2)

    def second(i, carry):
        cols = pl.ds(pl.multiple_of(i * tile, tile), tile)
        down = adapter[0, :, cols]
        gain = gain_ref[:, cols].astype(F32)
        unit = (x[:, :, cols].astype(F32).reshape(rows, tile) - mean) * inv
        scaled = jnp.dot(grad_pre, down, preferred_element_type=F32) * gain
        ups = upstream[:, cols]
        result = ups.astype(F32) + inv * (scaled - mean_v - unit * mean_vu)
        result = result.reshape(slots, rows_each, tile).astype(BF16)
        for j in range(slots):
            grads[targets[j], :, cols] = result[j]
        return carry

    lax.fori_loop(0, features // tile, second, 0, unroll=True)
    copies = []
    for k, load in enumerate(loads.values()):
        for i, (hop, cross) in enumerate(load):
            source = grads.at[pl.ds(4 * hop + 2 * cross, 2)]
            pair = 2 * hop + cross
            copies.append(pltpu.make_async_copy(source, grads_out[k].at[pl.ds(2 * i, 2)], out_sem.at[pair]))
    for copy in copies:
        copy.start()
    grad_pre_t = grad_pre_full.T.astype(BF16)
    hidden_t = act_value.T.astype(BF16)

    def third(i, carry):
        cols = pl.ds(pl.multiple_of(i * tile, tile), tile)
        grad_down = jnp.dot(grad_pre_t, normed[:, cols], preferred_element_type=F32)
        grad_up = jnp.dot(hidden_t, upstream[:, cols], preferred_element_type=F32)
        steps[0, :, cols] = (adapter[0, :, cols].astype(F32) - rate_down * grad_down).astype(BF16)
        steps[1, :, cols] = (adapter[1, :, cols].astype(F32) - rate_up * grad_up).astype(BF16)
        return carry

    lax.fori_loop(0, features // tile, third, 0, unroll=True)
    copies.append(pltpu.make_async_copy(steps, steps_out, out_sem.at[trips]))
    copies[-1].start()
    for copy in copies:
        copy.wait()


def step(outer_total, saved, incoming, gain, adapter, wiring, counts):
    slots, rows_each, features = saved.shape
    units = adapter.shape[1]
    rows = slots * rows_each
    loads = load_ranges(outer_total)
    count = len(loads)
    trips = 2 * outer_total
    parts = 4 if slots % 4 == 0 else 1
    hbm = pl.BlockSpec(memory_space=pl.ANY)
    results = pl.pallas_call(
        functools.partial(step_kernel, outer_total),
        out_shape=[jax.ShapeDtypeStruct((2 * len(load), rows_each, features), BF16) for load in loads.values()]
        + [jax.ShapeDtypeStruct((2, units, features), BF16)],
        in_specs=[hbm] * 6,
        out_specs=[hbm] * (count + 1),
        scratch_shapes=[
            pltpu.SMEM(wiring.shape, jnp.int32),
            pltpu.SMEM(counts.shape, jnp.int32),
            pltpu.VMEM(gain.shape, BF16),
            pltpu.VMEM((slots, rows_each, features), BF16),
            pltpu.VMEM((slots, rows_each, features), BF16),
            pltpu.VMEM((2, units, features), BF16),
            pltpu.VMEM((rows, features), BF16),
            pltpu.VMEM((rows, features), BF16),
            pltpu.VMEM((2 * trips, rows_each, features), BF16),
            pltpu.VMEM((2, units, features), BF16),
            pltpu.VMEM((rows, 128), F32),
            pltpu.VMEM((rows, 128), F32),
            pltpu.SemaphoreType.DMA((parts,)),
            pltpu.SemaphoreType.DMA((5,)),
            pltpu.SemaphoreType.DMA((trips + 1,)),
        ],
        compiler_params=pltpu.CompilerParams(vmem_limit_bytes=VMEM_BYTES),
        cost_estimate=pl.CostEstimate(
            flops=10 * rows * units * features, bytes_accessed=10 * rows * features, transcendentals=0
        ),
    )(wiring, counts, saved, incoming, gain, adapter)
    return dict(zip(loads, results[:count])), results[count]


def place_jobs(outer_total, trips, across, places_ref, blocks):
    outer, side, core = split_peer(lax.axis_index("peer"))
    jobs = []
    for (hop, cross), block in zip(trips, blocks):
        source_outer = lax.rem(outer - hop + outer_total, outer_total)
        source = source_outer * 4 + (side + cross) % 2 * 2
        target = places_ref[source + (1 - core if across else core)]
        jobs.append((target >= 0, target, block))
    return jobs


def run_jobs(jobs, out, sem, act):
    slots = out.shape[0]
    for index, (there, target, block) in enumerate(jobs):
        copy = pltpu.make_async_copy(block, out.at[jnp.clip(target, 0, slots - 1)], sem.at[index])
        pl.when(there)(copy.start if act == "start" else copy.wait)


def kept_kernel(outer_total, trips, places_ref, *rest):
    kept = rest[: len(trips)]
    sources = rest[len(trips) : len(trips) + 3]
    out, mean_out, one, two, three, mean, blank, sem, load_sem, store_sem = rest[len(trips) + 3 :]
    bands = load_sem.shape[1]
    rows = mean.shape[1]
    each = mean.shape[0] * rows // bands

    def band(ref, i):
        return ref.at[i * each // rows, pl.ds(i * each % rows, each)]

    loads = [
        [
            pltpu.make_async_copy(band(source, i), band(target, i), load_sem.at[k, i])
            for k, (source, target) in enumerate(zip(sources, (one, two, three)))
        ]
        for i in range(bands)
    ]
    for copies in loads:
        for copy in copies:
            copy.start()
    blank[...] = jnp.zeros_like(blank)
    jobs = place_jobs(outer_total, trips, False, places_ref, [part.at[0] for part in kept])
    arrived = places_ref[4 * outer_total]
    jobs += [(j >= arrived, j, blank) for j in range(out.shape[0])]
    run_jobs(jobs, out, sem, "start")
    stores = []
    for i in range(bands):
        for copy in loads[i]:
            copy.wait()
        total = band(one, i)[...].astype(F32) + band(two, i)[...].astype(F32) + band(three, i)[...].astype(F32)
        band(mean, i)[...] = (total * (1.0 / 3.0)).astype(BF16)
        stores.append(pltpu.make_async_copy(band(mean, i), band(mean_out, i), store_sem.at[i]))
        stores[-1].start()
    for copy in stores:
        copy.wait()
    run_jobs(jobs, out, sem, "wait")


def crossed_kernel(outer_total, trips, places_ref, crossed, _, out, sem):
    blocks = [crossed.at[k] for k in range(len(trips))]
    jobs = place_jobs(outer_total, trips, True, places_ref, blocks)
    run_jobs(jobs, out, sem, "start")
    run_jobs(jobs, out, sem, "wait")


def place_kept(outer_total, trips, places, kept, adapters, slots):
    vmem = pl.BlockSpec(memory_space=pltpu.VMEM)
    hbm = pl.BlockSpec(memory_space=pl.ANY)
    block = kept[0].shape[1:]
    whole = adapters[0].shape
    bands = whole[0] * whole[1] // BAND
    return pl.pallas_call(
        functools.partial(kept_kernel, outer_total, trips),
        out_shape=(jax.ShapeDtypeStruct((slots,) + block, BF16), jax.ShapeDtypeStruct(whole, BF16)),
        in_specs=[pl.BlockSpec(memory_space=pltpu.SMEM)] + [vmem] * len(kept) + [hbm] * 3,
        out_specs=(hbm, hbm),
        scratch_shapes=[pltpu.VMEM(whole, BF16)] * 4
        + [
            pltpu.VMEM(block, BF16),
            pltpu.SemaphoreType.DMA((len(trips) + slots,)),
            pltpu.SemaphoreType.DMA((3, bands)),
            pltpu.SemaphoreType.DMA((bands,)),
        ],
        compiler_params=pltpu.CompilerParams(vmem_limit_bytes=24 * 1024 * 1024),
        cost_estimate=pl.CostEstimate(
            flops=0, bytes_accessed=8 * whole[0] * whole[1] * whole[2], transcendentals=0
        ),
    )(places, *kept, *adapters)


def place_crossed(outer_total, trips, places, crossed, base):
    hbm = pl.BlockSpec(memory_space=pl.ANY)
    return pl.pallas_call(
        functools.partial(crossed_kernel, outer_total, trips),
        out_shape=jax.ShapeDtypeStruct(base.shape, BF16),
        in_specs=[
            pl.BlockSpec(memory_space=pltpu.SMEM),
            pl.BlockSpec(memory_space=pltpu.VMEM),
            hbm,
        ],
        out_specs=hbm,
        scratch_shapes=[pltpu.SemaphoreType.DMA((len(trips),))],
        input_output_aliases={2: 0},
        cost_estimate=pl.CostEstimate(flops=0, bytes_accessed=4 * crossed.size, transcendentals=0),
    )(places, crossed, base)


def arrival_places(section, peer, section_total, wiring, counts):
    sender_section = jnp.minimum(section + 1, section_total - 1)
    slot_ids = jnp.arange(wiring.shape[2], dtype=jnp.int32)
    active = slot_ids[None, :] < counts[sender_section][:, None]
    sends = jnp.any((wiring[sender_section] == peer) & active, axis=1) & (section + 1 < section_total)
    sends = sends.astype(jnp.int32)
    ids = jnp.arange(sends.shape[0], dtype=jnp.int32)
    earlier = jnp.sum(jnp.where(ids[None, :] < ids[:, None], sends[None, :], 0), axis=1)
    places = jnp.where(sends > 0, earlier, -1)
    return jnp.concatenate([places, jnp.sum(sends)[None]])


def peer_index(outer, side, core):
    return outer * 4 + side * 2 + core


def trip_pairs(section_total, outer_total, hop, cross, source_down, target_down):
    peers = 4 * outer_total
    pairs = []
    for section in range(1, section_total):
        for outer in range(outer_total):
            for side in range(2):
                for core in range(2):
                    source = (section - source_down) * peers + peer_index(outer, side, core)
                    target = peer_index((outer + hop) % outer_total, side ^ cross, core)
                    pairs.append((source, (section - target_down) * peers + target))
    return pairs


def after(value, *others):
    return lax.optimization_barrier((value,) + others)[0]


def exchange(blocks, stepped, places, peer_total, section_total, slots):
    outer_total = peer_total // 4
    partner = [(p, p ^ 1) for p in range(peer_total)]
    beyond = [(p, (p + 2 * (p % 2) - 1) % peer_total) for p in range(peer_total)]
    loads = load_ranges(outer_total)
    done = {}
    started = []
    for trip in expand(outer_total):
        name, hop, cross = trip
        pairs = functools.partial(trip_pairs, section_total, outer_total)
        if name in ("near", "far"):
            done[name] = lax.ppermute(stepped, "peer", partner if name == "near" else beyond)
            continue
        if name == "lift":
            block, pairs = blocks[name], pairs(0, 0, 0, 1)
        elif name == "swap":
            block, pairs = blocks[name], pairs(0, 1, 0, 0)
        elif name == "d":
            block, pairs = blocks[hop, cross], pairs(hop, cross, 0, 1)
        else:
            held = "lift" if name == "z" else "swap"
            first = 2 * loads[held].index((hop, cross))
            block = done[held][first : first + 2]
            pairs = pairs(hop, cross, 1, 1) if name == "z" else pairs(hop, 0, 0, 1)
        if len(started) == AHEAD - 1:
            block = after(block, done["near"])
        elif len(started) >= AHEAD:
            block = after(block, started[len(started) - AHEAD])
        held = name if name in ("lift", "swap") else (hop, cross)
        done[held] = lax.ppermute(block, AXES, pairs)
        started.append(done[held])
    trips = [(hop, cross) for name, hop, cross in expand(outer_total) if name in "dzr"]
    arrived = [done[trip] for trip in trips]
    crossing = jnp.concatenate([part[1:] for part in arrived])
    near, far = done["near"], done["far"]
    crossing, near, far, places = lax.optimization_barrier((crossing, near, far, places))
    crossed = lax.ppermute(crossing, "peer", partner)
    kept = [part[:1] for part in arrived]
    routed, averaged = place_kept(outer_total, trips, places, kept, (near, stepped, far), slots)
    routed = place_crossed(outer_total, trips, places, crossed, routed)
    return routed, averaged


def per_device(saved_inputs, incoming, norm_gain, adapter, wiring, counts):
    peer_total = lax.axis_size("peer")
    section_total = lax.axis_size("section")
    outer_total = peer_total // 4
    section, peer = lax.axis_index("section"), lax.axis_index("peer")
    slots = saved_inputs.shape[2]
    blocks, stepped = step(
        outer_total, saved_inputs[0, 0], incoming[0, 0], norm_gain[0], adapter[0, 0], wiring, counts
    )
    places = arrival_places(section, peer, section_total, wiring, counts)
    routed, averaged = exchange(blocks, stepped, places, peer_total, section_total, slots)
    return (routed[None, None], averaged[None, None])


def solution(mesh):
    return jax.shard_map(
        per_device,
        mesh=mesh,
        in_specs=(
            P("section", "peer", None, None, None),
            P("section", "peer", None, None, None),
            P("section", "peer", None),
            P("section", "peer", None, None, None),
            P(),
            P(),
        ),
        out_specs=(P("section", "peer", None, None, None), P("section", "peer", None, None, None)),
        check_vma=False,
    )
```

```python
import functools

import jax
import jax.numpy as jnp
from jax import lax
from jax.experimental import pallas as pl
from jax.experimental.pallas import tpu as pltpu
from jax.sharding import PartitionSpec as P

norm_eps = 1e-05
rate_down = 5e-05
rate_up = 0.003
inner_dims = (((1,), (1,)), ((), ()))
AXES = ("section", "peer")
TILE = 3584
AHEAD = 4
BAND = 64
ORDER = ("near", "far", "lift", "d00", "d31", "d30", "z20", "d11", "z21", "d01", "d10")
VMEM_BYTES = 60 * 1024 * 1024
F32 = jnp.float32
BF16 = jnp.bfloat16


def column_tile(features):
    return TILE if features % TILE == 0 else 128


def split_peer(peer):
    return peer // 4, (peer // 2) % 2, peer % 2


def expand(outer_total):
    relayed = outer_total // 2
    hops = {"0": [0], "1": range(1, relayed), "2": [relayed], "3": range(relayed + 1, outer_total)}
    order = []
    for name in ORDER:
        if name in ("near", "far", "lift", "swap"):
            order.append((name, 0, 0))
        else:
            order += [(name[0], hop, int(name[2])) for hop in hops[name[1]]]
    return order


def load_ranges(outer_total):
    order = expand(outer_total)
    loads = {}
    for name, hop, cross in order:
        if name == "lift":
            loads["lift"] = [(h, c) for n, h, c in order if n == "z"]
        if name == "swap":
            loads["swap"] = [(h, c) for n, h, c in order if n == "r"]
        if name == "d":
            loads[hop, cross] = [(hop, cross)]
    return loads


def step_kernel(outer_total, wiring_hbm, counts_hbm, x_hbm, g_hbm, gain_hbm, adapter_hbm, *rest):
    loads = load_ranges(outer_total)
    trips, count = 2 * outer_total, len(loads)
    grads_out = rest[:count]
    steps_out = rest[count]
    (wiring_ref, counts_ref, gain_ref, x, g, adapter, normed, upstream, grads, steps, mean_s, inv_s) = rest[
        count + 1 : count + 13
    ]
    x_sem, in_sem, out_sem = rest[count + 13 :]
    slots, rows_each, features = x.shape
    rows = slots * rows_each
    section, peer = lax.axis_index("section"), lax.axis_index("peer")
    outer, side, core = split_peer(peer)
    parts = x_sem.shape[0]
    each = slots // parts
    tile = column_tile(features)

    x_copies = [
        pltpu.make_async_copy(x_hbm.at[pl.ds(i * each, each)], x.at[pl.ds(i * each, each)], x_sem.at[i])
        for i in range(parts)
    ]
    for copy in x_copies:
        copy.start()
    small_copies = [
        pltpu.make_async_copy(source, target, in_sem.at[2 + i])
        for i, (source, target) in enumerate(
            ((wiring_hbm, wiring_ref), (counts_hbm, counts_ref), (gain_hbm, gain_ref))
        )
    ]
    for copy in small_copies:
        copy.start()
    adapter_copy = pltpu.make_async_copy(adapter_hbm, adapter, in_sem.at[0])
    adapter_copy.start()
    g_copy = pltpu.make_async_copy(g_hbm, g, in_sem.at[1])
    g_copy.start()

    def stats(slot):
        block = x[slot].astype(F32)
        mean = jnp.mean(block, axis=1, keepdims=True)
        centred = block - mean
        var = jnp.mean(centred * centred, axis=1, keepdims=True)
        row = pl.ds(pl.multiple_of(slot * rows_each, rows_each), rows_each)
        mean_s[row, :] = jnp.broadcast_to(mean, (rows_each, 128))
        inv_s[row, :] = jnp.broadcast_to(lax.rsqrt(var + norm_eps), (rows_each, 128))

    for i in range(parts):
        x_copies[i].wait()
        for j in range(each):
            stats(i * each + j)

    for copy in small_copies:
        copy.wait()
    mean = mean_s[:, :1]
    inv = inv_s[:, :1]
    live = lax.broadcasted_iota(jnp.int32, (rows, 1), 0) < counts_ref[section, peer] * rows_each

    adapter_copy.wait()
    g_copy.wait()

    def first(i, carry):
        pre, pulled, gained = carry
        cols = pl.ds(pl.multiple_of(i * tile, tile), tile)
        unit = (x[:, :, cols].astype(F32).reshape(rows, tile) - mean) * inv
        gain = gain_ref[:, cols].astype(F32)
        scaled = (unit * gain).astype(BF16)
        normed[:, cols] = scaled
        ups = jnp.where(live, g[:, :, cols].astype(F32).reshape(rows, tile), 0.0).astype(BF16)
        upstream[:, cols] = ups
        down = adapter[0, :, cols]
        pre = pre + lax.dot_general(scaled, down, inner_dims, preferred_element_type=F32)
        pulled = pulled + lax.dot_general(ups, adapter[1, :, cols], inner_dims, preferred_element_type=F32)
        gained = gained + jnp.sum(down.astype(F32) * gain, axis=1, keepdims=True)
        return pre, pulled, gained

    hidden_units = adapter.shape[1]
    zero = jnp.zeros((rows, hidden_units), F32)
    pre_act, grad_hidden, gained = lax.fori_loop(
        0, features // tile, first, (zero, zero, jnp.zeros((hidden_units, 1), F32)), unroll=True
    )
    act_value, act_pull = jax.vjp(jax.nn.gelu, pre_act)
    grad_pre = act_pull(grad_hidden)[0].astype(BF16)
    grad_pre_full = grad_pre.astype(F32)
    mean_v = jnp.sum(grad_pre_full * jnp.broadcast_to(gained, (hidden_units, rows)).T, axis=1, keepdims=True) / features
    mean_vu = jnp.sum(grad_pre_full * pre_act, axis=1, keepdims=True) / features

    targets = []
    for j in range(slots):
        outer_to, side_to, core_to = split_peer(wiring_ref[section, peer, j])
        hop = lax.rem(outer_to - outer + outer_total, outer_total)
        targets.append((hop * 2 + (side_to + side) % 2) * 2 + (core_to + core) % 2)

    def second(i, carry):
        cols = pl.ds(pl.multiple_of(i * tile, tile), tile)
        down = adapter[0, :, cols]
        gain = gain_ref[:, cols].astype(F32)
        unit = (x[:, :, cols].astype(F32).reshape(rows, tile) - mean) * inv
        scaled = jnp.dot(grad_pre, down, preferred_element_type=F32) * gain
        ups = upstream[:, cols]
        result = ups.astype(F32) + inv * (scaled - mean_v - unit * mean_vu)
        result = result.reshape(slots, rows_each, tile).astype(BF16)
        for j in range(slots):
            grads[targets[j], :, cols] = result[j]
        return carry

    lax.fori_loop(0, features // tile, second, 0, unroll=True)
    copies = []
    for k, load in enumerate(loads.values()):
        for i, (hop, cross) in enumerate(load):
            source = grads.at[pl.ds(4 * hop + 2 * cross, 2)]
            pair = 2 * hop + cross
            copies.append(pltpu.make_async_copy(source, grads_out[k].at[pl.ds(2 * i, 2)], out_sem.at[pair]))
    for copy in copies:
        copy.start()
    grad_pre_t = grad_pre_full.T.astype(BF16)
    hidden_t = act_value.T.astype(BF16)

    def third(i, carry):
        cols = pl.ds(pl.multiple_of(i * tile, tile), tile)
        grad_down = jnp.dot(grad_pre_t, normed[:, cols], preferred_element_type=F32)
        grad_up = jnp.dot(hidden_t, upstream[:, cols], preferred_element_type=F32)
        steps[0, :, cols] = (adapter[0, :, cols].astype(F32) - rate_down * grad_down).astype(BF16)
        steps[1, :, cols] = (adapter[1, :, cols].astype(F32) - rate_up * grad_up).astype(BF16)
        return carry

    lax.fori_loop(0, features // tile, third, 0, unroll=True)
    copies.append(pltpu.make_async_copy(steps, steps_out, out_sem.at[trips]))
    copies[-1].start()
    for copy in copies:
        copy.wait()


def step(outer_total, saved, incoming, gain, adapter, wiring, counts):
    slots, rows_each, features = saved.shape
    units = adapter.shape[1]
    rows = slots * rows_each
    loads = load_ranges(outer_total)
    count = len(loads)
    trips = 2 * outer_total
    parts = 4 if slots % 4 == 0 else 1
    hbm = pl.BlockSpec(memory_space=pl.ANY)
    results = pl.pallas_call(
        functools.partial(step_kernel, outer_total),
        out_shape=[jax.ShapeDtypeStruct((2 * len(load), rows_each, features), BF16) for load in loads.values()]
        + [jax.ShapeDtypeStruct((2, units, features), BF16)],
        in_specs=[hbm] * 6,
        out_specs=[hbm] * (count + 1),
        scratch_shapes=[
            pltpu.SMEM(wiring.shape, jnp.int32),
            pltpu.SMEM(counts.shape, jnp.int32),
            pltpu.VMEM(gain.shape, BF16),
            pltpu.VMEM((slots, rows_each, features), BF16),
            pltpu.VMEM((slots, rows_each, features), BF16),
            pltpu.VMEM((2, units, features), BF16),
            pltpu.VMEM((rows, features), BF16),
            pltpu.VMEM((rows, features), BF16),
            pltpu.VMEM((2 * trips, rows_each, features), BF16),
            pltpu.VMEM((2, units, features), BF16),
            pltpu.VMEM((rows, 128), F32),
            pltpu.VMEM((rows, 128), F32),
            pltpu.SemaphoreType.DMA((parts,)),
            pltpu.SemaphoreType.DMA((5,)),
            pltpu.SemaphoreType.DMA((trips + 1,)),
        ],
        compiler_params=pltpu.CompilerParams(vmem_limit_bytes=VMEM_BYTES),
        cost_estimate=pl.CostEstimate(
            flops=10 * rows * units * features, bytes_accessed=10 * rows * features, transcendentals=0
        ),
    )(wiring, counts, saved, incoming, gain, adapter)
    return dict(zip(loads, results[:count])), results[count]


def place_jobs(outer_total, trips, across, places_ref, blocks):
    outer, side, core = split_peer(lax.axis_index("peer"))
    jobs = []
    for (hop, cross), block in zip(trips, blocks):
        source_outer = lax.rem(outer - hop + outer_total, outer_total)
        source = source_outer * 4 + (side + cross) % 2 * 2
        target = places_ref[source + (1 - core if across else core)]
        jobs.append((target >= 0, target, block))
    return jobs


def run_jobs(jobs, out, sem, act):
    slots = out.shape[0]
    for index, (there, target, block) in enumerate(jobs):
        copy = pltpu.make_async_copy(block, out.at[jnp.clip(target, 0, slots - 1)], sem.at[index])
        pl.when(there)(copy.start if act == "start" else copy.wait)


def kept_kernel(outer_total, trips, places_ref, *rest):
    kept = rest[: len(trips)]
    sources = rest[len(trips) : len(trips) + 3]
    out, mean_out, one, two, three, mean, blank, sem, load_sem, store_sem = rest[len(trips) + 3 :]
    bands = load_sem.shape[1]
    rows = mean.shape[1]
    each = mean.shape[0] * rows // bands

    def band(ref, i):
        return ref.at[i * each // rows, pl.ds(i * each % rows, each)]

    loads = [
        [
            pltpu.make_async_copy(band(source, i), band(target, i), load_sem.at[k, i])
            for k, (source, target) in enumerate(zip(sources, (one, two, three)))
        ]
        for i in range(bands)
    ]
    for copies in loads:
        for copy in copies:
            copy.start()
    blank[...] = jnp.zeros_like(blank)
    jobs = place_jobs(outer_total, trips, False, places_ref, [part.at[0] for part in kept])
    arrived = places_ref[4 * outer_total]
    jobs += [(j >= arrived, j, blank) for j in range(out.shape[0])]
    run_jobs(jobs, out, sem, "start")
    stores = []
    for i in range(bands):
        for copy in loads[i]:
            copy.wait()
        total = band(one, i)[...].astype(F32) + band(two, i)[...].astype(F32) + band(three, i)[...].astype(F32)
        band(mean, i)[...] = (total * (1.0 / 3.0)).astype(BF16)
        stores.append(pltpu.make_async_copy(band(mean, i), band(mean_out, i), store_sem.at[i]))
        stores[-1].start()
    for copy in stores:
        copy.wait()
    run_jobs(jobs, out, sem, "wait")


def crossed_kernel(outer_total, trips, places_ref, crossed, _, out, sem):
    blocks = [crossed.at[k] for k in range(len(trips))]
    jobs = place_jobs(outer_total, trips, True, places_ref, blocks)
    run_jobs(jobs, out, sem, "start")
    run_jobs(jobs, out, sem, "wait")


def place_kept(outer_total, trips, places, kept, adapters, slots):
    vmem = pl.BlockSpec(memory_space=pltpu.VMEM)
    hbm = pl.BlockSpec(memory_space=pl.ANY)
    block = kept[0].shape[1:]
    whole = adapters[0].shape
    bands = whole[0] * whole[1] // BAND
    return pl.pallas_call(
        functools.partial(kept_kernel, outer_total, trips),
        out_shape=(jax.ShapeDtypeStruct((slots,) + block, BF16), jax.ShapeDtypeStruct(whole, BF16)),
        in_specs=[pl.BlockSpec(memory_space=pltpu.SMEM)] + [vmem] * len(kept) + [hbm] * 3,
        out_specs=(hbm, hbm),
        scratch_shapes=[pltpu.VMEM(whole, BF16)] * 4
        + [
            pltpu.VMEM(block, BF16),
            pltpu.SemaphoreType.DMA((len(trips) + slots,)),
            pltpu.SemaphoreType.DMA((3, bands)),
            pltpu.SemaphoreType.DMA((bands,)),
        ],
        compiler_params=pltpu.CompilerParams(vmem_limit_bytes=24 * 1024 * 1024),
        cost_estimate=pl.CostEstimate(
            flops=0, bytes_accessed=8 * whole[0] * whole[1] * whole[2], transcendentals=0
        ),
    )(places, *kept, *adapters)


def place_crossed(outer_total, trips, places, crossed, base):
    hbm = pl.BlockSpec(memory_space=pl.ANY)
    return pl.pallas_call(
        functools.partial(crossed_kernel, outer_total, trips),
        out_shape=jax.ShapeDtypeStruct(base.shape, BF16),
        in_specs=[
            pl.BlockSpec(memory_space=pltpu.SMEM),
            pl.BlockSpec(memory_space=pltpu.VMEM),
            hbm,
        ],
        out_specs=hbm,
        scratch_shapes=[pltpu.SemaphoreType.DMA((len(trips),))],
        input_output_aliases={2: 0},
        cost_estimate=pl.CostEstimate(flops=0, bytes_accessed=4 * crossed.size, transcendentals=0),
    )(places, crossed, base)


def arrival_places(section, peer, section_total, wiring, counts):
    sender_section = jnp.minimum(section + 1, section_total - 1)
    slot_ids = jnp.arange(wiring.shape[2], dtype=jnp.int32)
    active = slot_ids[None, :] < counts[sender_section][:, None]
    sends = jnp.any((wiring[sender_section] == peer) & active, axis=1) & (section + 1 < section_total)
    sends = sends.astype(jnp.int32)
    ids = jnp.arange(sends.shape[0], dtype=jnp.int32)
    earlier = jnp.sum(jnp.where(ids[None, :] < ids[:, None], sends[None, :], 0), axis=1)
    places = jnp.where(sends > 0, earlier, -1)
    return jnp.concatenate([places, jnp.sum(sends)[None]])


def peer_index(outer, side, core):
    return outer * 4 + side * 2 + core


def trip_pairs(section_total, outer_total, hop, cross, source_down, target_down):
    peers = 4 * outer_total
    pairs = []
    for section in range(1, section_total):
        for outer in range(outer_total):
            for side in range(2):
                for core in range(2):
                    source = (section - source_down) * peers + peer_index(outer, side, core)
                    target = peer_index((outer + hop) % outer_total, side ^ cross, core)
                    pairs.append((source, (section - target_down) * peers + target))
    return pairs


def after(value, *others):
    return lax.optimization_barrier((value,) + others)[0]


def exchange(blocks, stepped, places, peer_total, section_total, slots):
    outer_total = peer_total // 4
    partner = [(p, p ^ 1) for p in range(peer_total)]
    beyond = [(p, (p + 2 * (p % 2) - 1) % peer_total) for p in range(peer_total)]
    loads = load_ranges(outer_total)
    done = {}
    started = []
    for trip in expand(outer_total):
        name, hop, cross = trip
        pairs = functools.partial(trip_pairs, section_total, outer_total)
        if name in ("near", "far"):
            done[name] = lax.ppermute(stepped, "peer", partner if name == "near" else beyond)
            continue
        if name == "lift":
            block, pairs = blocks[name], pairs(0, 0, 0, 1)
        elif name == "swap":
            block, pairs = blocks[name], pairs(0, 1, 0, 0)
        elif name == "d":
            block, pairs = blocks[hop, cross], pairs(hop, cross, 0, 1)
        else:
            held = "lift" if name == "z" else "swap"
            first = 2 * loads[held].index((hop, cross))
            block = done[held][first : first + 2]
            pairs = pairs(hop, cross, 1, 1) if name == "z" else pairs(hop, 0, 0, 1)
        if len(started) == AHEAD - 1:
            block = after(block, done["near"])
        elif len(started) >= AHEAD:
            block = after(block, started[len(started) - AHEAD])
        held = name if name in ("lift", "swap") else (hop, cross)
        done[held] = lax.ppermute(block, AXES, pairs)
        started.append(done[held])
    trips = [(hop, cross) for name, hop, cross in expand(outer_total) if name in "dzr"]
    arrived = [done[trip] for trip in trips]
    crossing = jnp.concatenate([part[1:] for part in arrived])
    near, far = done["near"], done["far"]
    crossing, near, far, places = lax.optimization_barrier((crossing, near, far, places))
    crossed = lax.ppermute(crossing, "peer", partner)
    kept = [part[:1] for part in arrived]
    routed, averaged = place_kept(outer_total, trips, places, kept, (near, stepped, far), slots)
    routed = place_crossed(outer_total, trips, places, crossed, routed)
    return routed, averaged


def per_device(saved_inputs, incoming, norm_gain, adapter, wiring, counts):
    peer_total = lax.axis_size("peer")
    section_total = lax.axis_size("section")
    outer_total = peer_total // 4
    section, peer = lax.axis_index("section"), lax.axis_index("peer")
    slots = saved_inputs.shape[2]
    blocks, stepped = step(
        outer_total, saved_inputs[0, 0], incoming[0, 0], norm_gain[0], adapter[0, 0], wiring, counts
    )
    places = arrival_places(section, peer, section_total, wiring, counts)
    routed, averaged = exchange(blocks, stepped, places, peer_total, section_total, slots)
    return (routed[None, None], averaged[None, None])


def solution(mesh):
    return jax.shard_map(
        per_device,
        mesh=mesh,
        in_specs=(
            P("section", "peer", None, None, None),
            P("section", "peer", None, None, None),
            P("section", "peer", None),
            P("section", "peer", None, None, None),
            P(),
            P(),
        ),
        out_specs=(P("section", "peer", None, None, None), P("section", "peer", None, None, None)),
        check_vma=False,
    )
```

```python
import functools

import jax
import jax.numpy as jnp
from jax import lax
from jax.experimental import pallas as pl
from jax.experimental.pallas import tpu as pltpu
from jax.sharding import PartitionSpec as P

norm_eps = 1e-05
rate_down = 5e-05
rate_up = 0.003
inner_dims = (((1,), (1,)), ((), ()))
AXES = ("section", "peer")
TILE = 3584
AHEAD = 4
BAND = 64
ORDER = ("near", "far", "lift", "d00", "d31", "d30", "z20", "d11", "z21", "d01", "d10")
VMEM_BYTES = 60 * 1024 * 1024
F32 = jnp.float32
BF16 = jnp.bfloat16


def column_tile(features):
    return TILE if features % TILE == 0 else 128


def split_peer(peer):
    return peer // 4, (peer // 2) % 2, peer % 2


def expand(outer_total):
    relayed = outer_total // 2
    hops = {"0": [0], "1": range(1, relayed), "2": [relayed], "3": range(relayed + 1, outer_total)}
    order = []
    for name in ORDER:
        if name in ("near", "far", "lift", "swap"):
            order.append((name, 0, 0))
        else:
            order += [(name[0], hop, int(name[2])) for hop in hops[name[1]]]
    return order


def load_ranges(outer_total):
    order = expand(outer_total)
    loads = {}
    for name, hop, cross in order:
        if name == "lift":
            loads["lift"] = [(h, c) for n, h, c in order if n == "z"]
        if name == "swap":
            loads["swap"] = [(h, c) for n, h, c in order if n == "r"]
        if name == "d":
            loads[hop, cross] = [(hop, cross)]
    return loads


def step_kernel(outer_total, wiring_hbm, counts_hbm, x_hbm, g_hbm, gain_hbm, adapter_hbm, *rest):
    loads = load_ranges(outer_total)
    trips, count = 2 * outer_total, len(loads)
    grads_out = rest[:count]
    steps_out = rest[count]
    (wiring_ref, counts_ref, gain_ref, x, g, adapter, normed, upstream, grads, steps, mean_s, inv_s) = rest[
        count + 1 : count + 13
    ]
    x_sem, in_sem, out_sem = rest[count + 13 :]
    slots, rows_each, features = x.shape
    rows = slots * rows_each
    section, peer = lax.axis_index("section"), lax.axis_index("peer")
    outer, side, core = split_peer(peer)
    parts = x_sem.shape[0]
    each = slots // parts
    tile = column_tile(features)

    x_copies = [
        pltpu.make_async_copy(x_hbm.at[pl.ds(i * each, each)], x.at[pl.ds(i * each, each)], x_sem.at[i])
        for i in range(parts)
    ]
    for copy in x_copies:
        copy.start()
    small_copies = [
        pltpu.make_async_copy(source, target, in_sem.at[2 + i])
        for i, (source, target) in enumerate(
            ((wiring_hbm, wiring_ref), (counts_hbm, counts_ref), (gain_hbm, gain_ref))
        )
    ]
    for copy in small_copies:
        copy.start()
    adapter_copy = pltpu.make_async_copy(adapter_hbm, adapter, in_sem.at[0])
    adapter_copy.start()
    g_copy = pltpu.make_async_copy(g_hbm, g, in_sem.at[1])
    g_copy.start()

    def stats(slot):
        block = x[slot].astype(F32)
        mean = jnp.mean(block, axis=1, keepdims=True)
        centred = block - mean
        var = jnp.mean(centred * centred, axis=1, keepdims=True)
        row = pl.ds(pl.multiple_of(slot * rows_each, rows_each), rows_each)
        mean_s[row, :] = jnp.broadcast_to(mean, (rows_each, 128))
        inv_s[row, :] = jnp.broadcast_to(lax.rsqrt(var + norm_eps), (rows_each, 128))

    for i in range(parts):
        x_copies[i].wait()
        for j in range(each):
            stats(i * each + j)

    for copy in small_copies:
        copy.wait()
    mean = mean_s[:, :1]
    inv = inv_s[:, :1]
    live = lax.broadcasted_iota(jnp.int32, (rows, 1), 0) < counts_ref[section, peer] * rows_each

    adapter_copy.wait()
    g_copy.wait()

    def first(i, carry):
        pre, pulled, gained = carry
        cols = pl.ds(pl.multiple_of(i * tile, tile), tile)
        unit = (x[:, :, cols].astype(F32).reshape(rows, tile) - mean) * inv
        gain = gain_ref[:, cols].astype(F32)
        scaled = (unit * gain).astype(BF16)
        normed[:, cols] = scaled
        ups = jnp.where(live, g[:, :, cols].astype(F32).reshape(rows, tile), 0.0).astype(BF16)
        upstream[:, cols] = ups
        down = adapter[0, :, cols]
        pre = pre + lax.dot_general(scaled, down, inner_dims, preferred_element_type=F32)
        pulled = pulled + lax.dot_general(ups, adapter[1, :, cols], inner_dims, preferred_element_type=F32)
        gained = gained + jnp.sum(down.astype(F32) * gain, axis=1, keepdims=True)
        return pre, pulled, gained

    hidden_units = adapter.shape[1]
    zero = jnp.zeros((rows, hidden_units), F32)
    pre_act, grad_hidden, gained = lax.fori_loop(
        0, features // tile, first, (zero, zero, jnp.zeros((hidden_units, 1), F32)), unroll=True
    )
    act_value, act_pull = jax.vjp(jax.nn.gelu, pre_act)
    grad_pre = act_pull(grad_hidden)[0].astype(BF16)
    grad_pre_full = grad_pre.astype(F32)
    mean_v = jnp.sum(grad_pre_full * jnp.broadcast_to(gained, (hidden_units, rows)).T, axis=1, keepdims=True) / features
    mean_vu = jnp.sum(grad_pre_full * pre_act, axis=1, keepdims=True) / features

    targets = []
    for j in range(slots):
        outer_to, side_to, core_to = split_peer(wiring_ref[section, peer, j])
        hop = lax.rem(outer_to - outer + outer_total, outer_total)
        targets.append((hop * 2 + (side_to + side) % 2) * 2 + (core_to + core) % 2)

    def second(i, carry):
        cols = pl.ds(pl.multiple_of(i * tile, tile), tile)
        down = adapter[0, :, cols]
        gain = gain_ref[:, cols].astype(F32)
        unit = (x[:, :, cols].astype(F32).reshape(rows, tile) - mean) * inv
        scaled = jnp.dot(grad_pre, down, preferred_element_type=F32) * gain
        ups = upstream[:, cols]
        result = ups.astype(F32) + inv * (scaled - mean_v - unit * mean_vu)
        result = result.reshape(slots, rows_each, tile).astype(BF16)
        for j in range(slots):
            grads[targets[j], :, cols] = result[j]
        return carry

    lax.fori_loop(0, features // tile, second, 0, unroll=True)
    copies = []
    for k, load in enumerate(loads.values()):
        for i, (hop, cross) in enumerate(load):
            source = grads.at[pl.ds(4 * hop + 2 * cross, 2)]
            pair = 2 * hop + cross
            copies.append(pltpu.make_async_copy(source, grads_out[k].at[pl.ds(2 * i, 2)], out_sem.at[pair]))
    for copy in copies:
        copy.start()
    grad_pre_t = grad_pre_full.T.astype(BF16)
    hidden_t = act_value.T.astype(BF16)

    def third(i, carry):
        cols = pl.ds(pl.multiple_of(i * tile, tile), tile)
        grad_down = jnp.dot(grad_pre_t, normed[:, cols], preferred_element_type=F32)
        grad_up = jnp.dot(hidden_t, upstream[:, cols], preferred_element_type=F32)
        steps[0, :, cols] = (adapter[0, :, cols].astype(F32) - rate_down * grad_down).astype(BF16)
        steps[1, :, cols] = (adapter[1, :, cols].astype(F32) - rate_up * grad_up).astype(BF16)
        return carry

    lax.fori_loop(0, features // tile, third, 0, unroll=True)
    copies.append(pltpu.make_async_copy(steps, steps_out, out_sem.at[trips]))
    copies[-1].start()
    for copy in copies:
        copy.wait()


def step(outer_total, saved, incoming, gain, adapter, wiring, counts):
    slots, rows_each, features = saved.shape
    units = adapter.shape[1]
    rows = slots * rows_each
    loads = load_ranges(outer_total)
    count = len(loads)
    trips = 2 * outer_total
    parts = 4 if slots % 4 == 0 else 1
    hbm = pl.BlockSpec(memory_space=pl.ANY)
    results = pl.pallas_call(
        functools.partial(step_kernel, outer_total),
        out_shape=[jax.ShapeDtypeStruct((2 * len(load), rows_each, features), BF16) for load in loads.values()]
        + [jax.ShapeDtypeStruct((2, units, features), BF16)],
        in_specs=[hbm] * 6,
        out_specs=[hbm] * (count + 1),
        scratch_shapes=[
            pltpu.SMEM(wiring.shape, jnp.int32),
            pltpu.SMEM(counts.shape, jnp.int32),
            pltpu.VMEM(gain.shape, BF16),
            pltpu.VMEM((slots, rows_each, features), BF16),
            pltpu.VMEM((slots, rows_each, features), BF16),
            pltpu.VMEM((2, units, features), BF16),
            pltpu.VMEM((rows, features), BF16),
            pltpu.VMEM((rows, features), BF16),
            pltpu.VMEM((2 * trips, rows_each, features), BF16),
            pltpu.VMEM((2, units, features), BF16),
            pltpu.VMEM((rows, 128), F32),
            pltpu.VMEM((rows, 128), F32),
            pltpu.SemaphoreType.DMA((parts,)),
            pltpu.SemaphoreType.DMA((5,)),
            pltpu.SemaphoreType.DMA((trips + 1,)),
        ],
        compiler_params=pltpu.CompilerParams(vmem_limit_bytes=VMEM_BYTES),
        cost_estimate=pl.CostEstimate(
            flops=10 * rows * units * features, bytes_accessed=10 * rows * features, transcendentals=0
        ),
    )(wiring, counts, saved, incoming, gain, adapter)
    return dict(zip(loads, results[:count])), results[count]


def place_jobs(outer_total, trips, across, places_ref, blocks):
    outer, side, core = split_peer(lax.axis_index("peer"))
    jobs = []
    for (hop, cross), block in zip(trips, blocks):
        source_outer = lax.rem(outer - hop + outer_total, outer_total)
        source = source_outer * 4 + (side + cross) % 2 * 2
        target = places_ref[source + (1 - core if across else core)]
        jobs.append((target >= 0, target, block))
    return jobs


def run_jobs(jobs, out, sem, act):
    slots = out.shape[0]
    for index, (there, target, block) in enumerate(jobs):
        copy = pltpu.make_async_copy(block, out.at[jnp.clip(target, 0, slots - 1)], sem.at[index])
        pl.when(there)(copy.start if act == "start" else copy.wait)


def kept_kernel(outer_total, trips, places_ref, *rest):
    kept = rest[: len(trips)]
    sources = rest[len(trips) : len(trips) + 3]
    out, mean_out, one, two, three, mean, blank, sem, load_sem, store_sem = rest[len(trips) + 3 :]
    bands = load_sem.shape[1]
    rows = mean.shape[1]
    each = mean.shape[0] * rows // bands

    def band(ref, i):
        return ref.at[i * each // rows, pl.ds(i * each % rows, each)]

    loads = [
        [
            pltpu.make_async_copy(band(source, i), band(target, i), load_sem.at[k, i])
            for k, (source, target) in enumerate(zip(sources, (one, two, three)))
        ]
        for i in range(bands)
    ]
    for copies in loads:
        for copy in copies:
            copy.start()
    blank[...] = jnp.zeros_like(blank)
    jobs = place_jobs(outer_total, trips, False, places_ref, [part.at[0] for part in kept])
    arrived = places_ref[4 * outer_total]
    jobs += [(j >= arrived, j, blank) for j in range(out.shape[0])]
    run_jobs(jobs, out, sem, "start")
    stores = []
    for i in range(bands):
        for copy in loads[i]:
            copy.wait()
        total = band(one, i)[...].astype(F32) + band(two, i)[...].astype(F32) + band(three, i)[...].astype(F32)
        band(mean, i)[...] = (total * (1.0 / 3.0)).astype(BF16)
        stores.append(pltpu.make_async_copy(band(mean, i), band(mean_out, i), store_sem.at[i]))
        stores[-1].start()
    for copy in stores:
        copy.wait()
    run_jobs(jobs, out, sem, "wait")


def crossed_kernel(outer_total, trips, places_ref, crossed, _, out, held, load_sem, sem):
    loads = [pltpu.make_async_copy(crossed.at[k], held.at[k], load_sem.at[k]) for k in range(len(trips))]
    for copy in loads:
        copy.start()
    jobs = place_jobs(outer_total, trips, True, places_ref, [held.at[k] for k in range(len(trips))])
    slots = out.shape[0]
    for index, (there, target, block) in enumerate(jobs):
        loads[index].wait()
        pl.when(there)(
            pltpu.make_async_copy(block, out.at[jnp.clip(target, 0, slots - 1)], sem.at[index]).start
        )
    run_jobs(jobs, out, sem, "wait")


def place_kept(outer_total, trips, places, kept, adapters, slots):
    vmem = pl.BlockSpec(memory_space=pltpu.VMEM)
    hbm = pl.BlockSpec(memory_space=pl.ANY)
    block = kept[0].shape[1:]
    whole = adapters[0].shape
    bands = whole[0] * whole[1] // BAND
    return pl.pallas_call(
        functools.partial(kept_kernel, outer_total, trips),
        out_shape=(jax.ShapeDtypeStruct((slots,) + block, BF16), jax.ShapeDtypeStruct(whole, BF16)),
        in_specs=[pl.BlockSpec(memory_space=pltpu.SMEM)] + [vmem] * len(kept) + [hbm] * 3,
        out_specs=(hbm, hbm),
        scratch_shapes=[pltpu.VMEM(whole, BF16)] * 4
        + [
            pltpu.VMEM(block, BF16),
            pltpu.SemaphoreType.DMA((len(trips) + slots,)),
            pltpu.SemaphoreType.DMA((3, bands)),
            pltpu.SemaphoreType.DMA((bands,)),
        ],
        compiler_params=pltpu.CompilerParams(vmem_limit_bytes=24 * 1024 * 1024),
        cost_estimate=pl.CostEstimate(
            flops=0, bytes_accessed=8 * whole[0] * whole[1] * whole[2], transcendentals=0
        ),
    )(places, *kept, *adapters)


def place_crossed(outer_total, trips, places, crossed, base):
    hbm = pl.BlockSpec(memory_space=pl.ANY)
    return pl.pallas_call(
        functools.partial(crossed_kernel, outer_total, trips),
        out_shape=jax.ShapeDtypeStruct(base.shape, BF16),
        in_specs=[
            pl.BlockSpec(memory_space=pltpu.SMEM),
            hbm,
            hbm,
        ],
        out_specs=hbm,
        scratch_shapes=[
            pltpu.VMEM(crossed.shape, BF16),
            pltpu.SemaphoreType.DMA((len(trips),)),
            pltpu.SemaphoreType.DMA((len(trips),)),
        ],
        input_output_aliases={2: 0},
        cost_estimate=pl.CostEstimate(flops=0, bytes_accessed=4 * crossed.size, transcendentals=0),
    )(places, crossed, base)


def arrival_places(section, peer, section_total, wiring, counts):
    sender_section = jnp.minimum(section + 1, section_total - 1)
    slot_ids = jnp.arange(wiring.shape[2], dtype=jnp.int32)
    active = slot_ids[None, :] < counts[sender_section][:, None]
    sends = jnp.any((wiring[sender_section] == peer) & active, axis=1) & (section + 1 < section_total)
    sends = sends.astype(jnp.int32)
    ids = jnp.arange(sends.shape[0], dtype=jnp.int32)
    earlier = jnp.sum(jnp.where(ids[None, :] < ids[:, None], sends[None, :], 0), axis=1)
    places = jnp.where(sends > 0, earlier, -1)
    return jnp.concatenate([places, jnp.sum(sends)[None]])


def peer_index(outer, side, core):
    return outer * 4 + side * 2 + core


def trip_pairs(section_total, outer_total, hop, cross, source_down, target_down):
    peers = 4 * outer_total
    pairs = []
    for section in range(1, section_total):
        for outer in range(outer_total):
            for side in range(2):
                for core in range(2):
                    source = (section - source_down) * peers + peer_index(outer, side, core)
                    target = peer_index((outer + hop) % outer_total, side ^ cross, core)
                    pairs.append((source, (section - target_down) * peers + target))
    return pairs


def after(value, *others):
    return lax.optimization_barrier((value,) + others)[0]


def exchange(blocks, stepped, places, peer_total, section_total, slots):
    outer_total = peer_total // 4
    partner = [(p, p ^ 1) for p in range(peer_total)]
    beyond = [(p, (p + 2 * (p % 2) - 1) % peer_total) for p in range(peer_total)]
    loads = load_ranges(outer_total)
    done = {}
    started = []
    for trip in expand(outer_total):
        name, hop, cross = trip
        pairs = functools.partial(trip_pairs, section_total, outer_total)
        if name in ("near", "far"):
            done[name] = lax.ppermute(stepped, "peer", partner if name == "near" else beyond)
            continue
        if name == "lift":
            block, pairs = blocks[name], pairs(0, 0, 0, 1)
        elif name == "swap":
            block, pairs = blocks[name], pairs(0, 1, 0, 0)
        elif name == "d":
            block, pairs = blocks[hop, cross], pairs(hop, cross, 0, 1)
        else:
            held = "lift" if name == "z" else "swap"
            first = 2 * loads[held].index((hop, cross))
            block = done[held][first : first + 2]
            pairs = pairs(hop, cross, 1, 1) if name == "z" else pairs(hop, 0, 0, 1)
        if len(started) == AHEAD - 1:
            block = after(block, done["near"])
        elif len(started) >= AHEAD:
            block = after(block, started[len(started) - AHEAD])
        held = name if name in ("lift", "swap") else (hop, cross)
        done[held] = lax.ppermute(block, AXES, pairs)
        started.append(done[held])
    trips = [(hop, cross) for name, hop, cross in expand(outer_total) if name in "dzr"]
    arrived = [done[trip] for trip in trips]
    crossing = jnp.concatenate([part[1:] for part in arrived])
    near, far = done["near"], done["far"]
    crossing, near, far, places = lax.optimization_barrier((crossing, near, far, places))
    crossed = lax.ppermute(crossing, "peer", partner)
    kept = [part[:1] for part in arrived]
    routed, averaged = place_kept(outer_total, trips, places, kept, (near, stepped, far), slots)
    routed = place_crossed(outer_total, trips, places, crossed, routed)
    return routed, averaged


def per_device(saved_inputs, incoming, norm_gain, adapter, wiring, counts):
    peer_total = lax.axis_size("peer")
    section_total = lax.axis_size("section")
    outer_total = peer_total // 4
    section, peer = lax.axis_index("section"), lax.axis_index("peer")
    slots = saved_inputs.shape[2]
    blocks, stepped = step(
        outer_total, saved_inputs[0, 0], incoming[0, 0], norm_gain[0], adapter[0, 0], wiring, counts
    )
    places = arrival_places(section, peer, section_total, wiring, counts)
    routed, averaged = exchange(blocks, stepped, places, peer_total, section_total, slots)
    return (routed[None, None], averaged[None, None])


def solution(mesh):
    return jax.shard_map(
        per_device,
        mesh=mesh,
        in_specs=(
            P("section", "peer", None, None, None),
            P("section", "peer", None, None, None),
            P("section", "peer", None),
            P("section", "peer", None, None, None),
            P(),
            P(),
        ),
        out_specs=(P("section", "peer", None, None, None), P("section", "peer", None, None, None)),
        check_vma=False,
    )
```

```python
import functools

import jax
import jax.numpy as jnp
from jax import lax
from jax.experimental import pallas as pl
from jax.experimental.pallas import tpu as pltpu
from jax.sharding import PartitionSpec as P

norm_eps = 1e-05
rate_down = 5e-05
rate_up = 0.003
inner_dims = (((1,), (1,)), ((), ()))
AXES = ("section", "peer")
TILE = 3584
AHEAD = 4
BAND = 64
ORDER = ("d00", "near", "lift", "d30", "z20", "d31", "d11", "z21", "far", "d01", "d10")
VMEM_BYTES = 60 * 1024 * 1024
F32 = jnp.float32
BF16 = jnp.bfloat16


def column_tile(features):
    return TILE if features % TILE == 0 else 128


def split_peer(peer):
    return peer // 4, (peer // 2) % 2, peer % 2


def expand(outer_total):
    relayed = outer_total // 2
    hops = {"0": [0], "1": range(1, relayed), "2": [relayed], "3": range(relayed + 1, outer_total)}
    order = []
    for name in ORDER:
        if name in ("near", "far", "lift", "swap"):
            order.append((name, 0, 0))
        else:
            order += [(name[0], hop, int(name[2])) for hop in hops[name[1]]]
    return order


def load_ranges(outer_total):
    order = expand(outer_total)
    loads = {}
    for name, hop, cross in order:
        if name == "lift":
            loads["lift"] = [(h, c) for n, h, c in order if n == "z"]
        if name == "swap":
            loads["swap"] = [(h, c) for n, h, c in order if n == "r"]
        if name == "d":
            loads[hop, cross] = [(hop, cross)]
    return loads


def step_kernel(outer_total, wiring_hbm, counts_hbm, x_hbm, g_hbm, gain_hbm, adapter_hbm, *rest):
    loads = load_ranges(outer_total)
    trips, count = 2 * outer_total, len(loads)
    grads_out = rest[:count]
    steps_out = rest[count]
    (wiring_ref, counts_ref, gain_ref, x, g, adapter, normed, upstream, grads, steps, mean_s, inv_s) = rest[
        count + 1 : count + 13
    ]
    x_sem, in_sem, out_sem = rest[count + 13 :]
    slots, rows_each, features = x.shape
    rows = slots * rows_each
    section, peer = lax.axis_index("section"), lax.axis_index("peer")
    outer, side, core = split_peer(peer)
    parts = x_sem.shape[0]
    each = slots // parts
    tile = column_tile(features)

    x_copies = [
        pltpu.make_async_copy(x_hbm.at[pl.ds(i * each, each)], x.at[pl.ds(i * each, each)], x_sem.at[i])
        for i in range(parts)
    ]
    for copy in x_copies:
        copy.start()
    small_copies = [
        pltpu.make_async_copy(source, target, in_sem.at[2 + i])
        for i, (source, target) in enumerate(
            ((wiring_hbm, wiring_ref), (counts_hbm, counts_ref), (gain_hbm, gain_ref))
        )
    ]
    for copy in small_copies:
        copy.start()
    adapter_copy = pltpu.make_async_copy(adapter_hbm, adapter, in_sem.at[0])
    adapter_copy.start()
    g_copy = pltpu.make_async_copy(g_hbm, g, in_sem.at[1])
    g_copy.start()

    def stats(slot):
        block = x[slot].astype(F32)
        mean = jnp.mean(block, axis=1, keepdims=True)
        centred = block - mean
        var = jnp.mean(centred * centred, axis=1, keepdims=True)
        row = pl.ds(pl.multiple_of(slot * rows_each, rows_each), rows_each)
        mean_s[row, :] = jnp.broadcast_to(mean, (rows_each, 128))
        inv_s[row, :] = jnp.broadcast_to(lax.rsqrt(var + norm_eps), (rows_each, 128))

    for i in range(parts):
        x_copies[i].wait()
        for j in range(each):
            stats(i * each + j)

    for copy in small_copies:
        copy.wait()
    mean = mean_s[:, :1]
    inv = inv_s[:, :1]
    live = lax.broadcasted_iota(jnp.int32, (rows, 1), 0) < counts_ref[section, peer] * rows_each

    adapter_copy.wait()
    g_copy.wait()

    def first(i, carry):
        pre, pulled, gained = carry
        cols = pl.ds(pl.multiple_of(i * tile, tile), tile)
        unit = (x[:, :, cols].astype(F32).reshape(rows, tile) - mean) * inv
        gain = gain_ref[:, cols].astype(F32)
        scaled = (unit * gain).astype(BF16)
        normed[:, cols] = scaled
        ups = jnp.where(live, g[:, :, cols].astype(F32).reshape(rows, tile), 0.0).astype(BF16)
        upstream[:, cols] = ups
        down = adapter[0, :, cols]
        pre = pre + lax.dot_general(scaled, down, inner_dims, preferred_element_type=F32)
        pulled = pulled + lax.dot_general(ups, adapter[1, :, cols], inner_dims, preferred_element_type=F32)
        gained = gained + jnp.sum(down.astype(F32) * gain, axis=1, keepdims=True)
        return pre, pulled, gained

    hidden_units = adapter.shape[1]
    zero = jnp.zeros((rows, hidden_units), F32)
    pre_act, grad_hidden, gained = lax.fori_loop(
        0, features // tile, first, (zero, zero, jnp.zeros((hidden_units, 1), F32)), unroll=True
    )
    act_value, act_pull = jax.vjp(jax.nn.gelu, pre_act)
    grad_pre = act_pull(grad_hidden)[0].astype(BF16)
    grad_pre_full = grad_pre.astype(F32)
    mean_v = jnp.sum(grad_pre_full * jnp.broadcast_to(gained, (hidden_units, rows)).T, axis=1, keepdims=True) / features
    mean_vu = jnp.sum(grad_pre_full * pre_act, axis=1, keepdims=True) / features

    targets = []
    for j in range(slots):
        outer_to, side_to, core_to = split_peer(wiring_ref[section, peer, j])
        hop = lax.rem(outer_to - outer + outer_total, outer_total)
        targets.append((hop * 2 + (side_to + side) % 2) * 2 + (core_to + core) % 2)

    def second(i, carry):
        cols = pl.ds(pl.multiple_of(i * tile, tile), tile)
        down = adapter[0, :, cols]
        gain = gain_ref[:, cols].astype(F32)
        unit = (x[:, :, cols].astype(F32).reshape(rows, tile) - mean) * inv
        scaled = jnp.dot(grad_pre, down, preferred_element_type=F32) * gain
        ups = upstream[:, cols]
        result = ups.astype(F32) + inv * (scaled - mean_v - unit * mean_vu)
        result = result.reshape(slots, rows_each, tile).astype(BF16)
        for j in range(slots):
            grads[targets[j], :, cols] = result[j]
        return carry

    lax.fori_loop(0, features // tile, second, 0, unroll=True)
    copies = []
    for k, load in enumerate(loads.values()):
        for i, (hop, cross) in enumerate(load):
            source = grads.at[pl.ds(4 * hop + 2 * cross, 2)]
            pair = 2 * hop + cross
            copies.append(pltpu.make_async_copy(source, grads_out[k].at[pl.ds(2 * i, 2)], out_sem.at[pair]))
    for copy in copies:
        copy.start()
    grad_pre_t = grad_pre_full.T.astype(BF16)
    hidden_t = act_value.T.astype(BF16)

    def third(i, carry):
        cols = pl.ds(pl.multiple_of(i * tile, tile), tile)
        grad_down = jnp.dot(grad_pre_t, normed[:, cols], preferred_element_type=F32)
        grad_up = jnp.dot(hidden_t, upstream[:, cols], preferred_element_type=F32)
        steps[0, :, cols] = (adapter[0, :, cols].astype(F32) - rate_down * grad_down).astype(BF16)
        steps[1, :, cols] = (adapter[1, :, cols].astype(F32) - rate_up * grad_up).astype(BF16)
        return carry

    lax.fori_loop(0, features // tile, third, 0, unroll=True)
    copies.append(pltpu.make_async_copy(steps, steps_out, out_sem.at[trips]))
    copies[-1].start()
    for copy in copies:
        copy.wait()


def step(outer_total, saved, incoming, gain, adapter, wiring, counts):
    slots, rows_each, features = saved.shape
    units = adapter.shape[1]
    rows = slots * rows_each
    loads = load_ranges(outer_total)
    count = len(loads)
    trips = 2 * outer_total
    parts = 4 if slots % 4 == 0 else 1
    hbm = pl.BlockSpec(memory_space=pl.ANY)
    results = pl.pallas_call(
        functools.partial(step_kernel, outer_total),
        out_shape=[jax.ShapeDtypeStruct((2 * len(load), rows_each, features), BF16) for load in loads.values()]
        + [jax.ShapeDtypeStruct((2, units, features), BF16)],
        in_specs=[hbm] * 6,
        out_specs=[hbm] * (count + 1),
        scratch_shapes=[
            pltpu.SMEM(wiring.shape, jnp.int32),
            pltpu.SMEM(counts.shape, jnp.int32),
            pltpu.VMEM(gain.shape, BF16),
            pltpu.VMEM((slots, rows_each, features), BF16),
            pltpu.VMEM((slots, rows_each, features), BF16),
            pltpu.VMEM((2, units, features), BF16),
            pltpu.VMEM((rows, features), BF16),
            pltpu.VMEM((rows, features), BF16),
            pltpu.VMEM((2 * trips, rows_each, features), BF16),
            pltpu.VMEM((2, units, features), BF16),
            pltpu.VMEM((rows, 128), F32),
            pltpu.VMEM((rows, 128), F32),
            pltpu.SemaphoreType.DMA((parts,)),
            pltpu.SemaphoreType.DMA((5,)),
            pltpu.SemaphoreType.DMA((trips + 1,)),
        ],
        compiler_params=pltpu.CompilerParams(vmem_limit_bytes=VMEM_BYTES),
        cost_estimate=pl.CostEstimate(
            flops=10 * rows * units * features, bytes_accessed=10 * rows * features, transcendentals=0
        ),
    )(wiring, counts, saved, incoming, gain, adapter)
    return dict(zip(loads, results[:count])), results[count]


def place_jobs(outer_total, trips, across, places_ref, blocks):
    outer, side, core = split_peer(lax.axis_index("peer"))
    jobs = []
    for (hop, cross), block in zip(trips, blocks):
        source_outer = lax.rem(outer - hop + outer_total, outer_total)
        source = source_outer * 4 + (side + cross) % 2 * 2
        target = places_ref[source + (1 - core if across else core)]
        jobs.append((target >= 0, target, block))
    return jobs


def run_jobs(jobs, out, sem, act):
    slots = out.shape[0]
    for index, (there, target, block) in enumerate(jobs):
        copy = pltpu.make_async_copy(block, out.at[jnp.clip(target, 0, slots - 1)], sem.at[index])
        pl.when(there)(copy.start if act == "start" else copy.wait)


def kept_kernel(outer_total, trips, places_ref, *rest):
    kept = rest[: len(trips)]
    sources = rest[len(trips) : len(trips) + 3]
    out, mean_out, one, two, three, mean, blank, sem, load_sem, store_sem = rest[len(trips) + 3 :]
    bands = load_sem.shape[1]
    rows = mean.shape[1]
    each = mean.shape[0] * rows // bands

    def band(ref, i):
        return ref.at[i * each // rows, pl.ds(i * each % rows, each)]

    loads = [
        [
            pltpu.make_async_copy(band(source, i), band(target, i), load_sem.at[k, i])
            for k, (source, target) in enumerate(zip(sources, (one, two, three)))
        ]
        for i in range(bands)
    ]
    for copies in loads:
        for copy in copies:
            copy.start()
    blank[...] = jnp.zeros_like(blank)
    jobs = place_jobs(outer_total, trips, False, places_ref, [part.at[0] for part in kept])
    arrived = places_ref[4 * outer_total]
    jobs += [(j >= arrived, j, blank) for j in range(out.shape[0])]
    run_jobs(jobs, out, sem, "start")
    stores = []
    for i in range(bands):
        for copy in loads[i]:
            copy.wait()
        total = band(one, i)[...].astype(F32) + band(two, i)[...].astype(F32) + band(three, i)[...].astype(F32)
        band(mean, i)[...] = (total * (1.0 / 3.0)).astype(BF16)
        stores.append(pltpu.make_async_copy(band(mean, i), band(mean_out, i), store_sem.at[i]))
        stores[-1].start()
    for copy in stores:
        copy.wait()
    run_jobs(jobs, out, sem, "wait")


def crossed_kernel(outer_total, trips, places_ref, crossed, _, out, sem):
    blocks = [crossed.at[k] for k in range(len(trips))]
    jobs = place_jobs(outer_total, trips, True, places_ref, blocks)
    run_jobs(jobs, out, sem, "start")
    run_jobs(jobs, out, sem, "wait")


def place_kept(outer_total, trips, places, kept, adapters, slots):
    vmem = pl.BlockSpec(memory_space=pltpu.VMEM)
    hbm = pl.BlockSpec(memory_space=pl.ANY)
    block = kept[0].shape[1:]
    whole = adapters[0].shape
    bands = whole[0] * whole[1] // BAND
    return pl.pallas_call(
        functools.partial(kept_kernel, outer_total, trips),
        out_shape=(jax.ShapeDtypeStruct((slots,) + block, BF16), jax.ShapeDtypeStruct(whole, BF16)),
        in_specs=[pl.BlockSpec(memory_space=pltpu.SMEM)] + [vmem] * len(kept) + [hbm] * 3,
        out_specs=(hbm, hbm),
        scratch_shapes=[pltpu.VMEM(whole, BF16)] * 4
        + [
            pltpu.VMEM(block, BF16),
            pltpu.SemaphoreType.DMA((len(trips) + slots,)),
            pltpu.SemaphoreType.DMA((3, bands)),
            pltpu.SemaphoreType.DMA((bands,)),
        ],
        compiler_params=pltpu.CompilerParams(vmem_limit_bytes=24 * 1024 * 1024),
        cost_estimate=pl.CostEstimate(
            flops=0, bytes_accessed=8 * whole[0] * whole[1] * whole[2], transcendentals=0
        ),
    )(places, *kept, *adapters)


def place_crossed(outer_total, trips, places, crossed, base):
    hbm = pl.BlockSpec(memory_space=pl.ANY)
    return pl.pallas_call(
        functools.partial(crossed_kernel, outer_total, trips),
        out_shape=jax.ShapeDtypeStruct(base.shape, BF16),
        in_specs=[
            pl.BlockSpec(memory_space=pltpu.SMEM),
            pl.BlockSpec(memory_space=pltpu.VMEM),
            hbm,
        ],
        out_specs=hbm,
        scratch_shapes=[pltpu.SemaphoreType.DMA((len(trips),))],
        input_output_aliases={2: 0},
        cost_estimate=pl.CostEstimate(flops=0, bytes_accessed=4 * crossed.size, transcendentals=0),
    )(places, crossed, base)


def arrival_places(section, peer, section_total, wiring, counts):
    sender_section = jnp.minimum(section + 1, section_total - 1)
    slot_ids = jnp.arange(wiring.shape[2], dtype=jnp.int32)
    active = slot_ids[None, :] < counts[sender_section][:, None]
    sends = jnp.any((wiring[sender_section] == peer) & active, axis=1) & (section + 1 < section_total)
    sends = sends.astype(jnp.int32)
    ids = jnp.arange(sends.shape[0], dtype=jnp.int32)
    earlier = jnp.sum(jnp.where(ids[None, :] < ids[:, None], sends[None, :], 0), axis=1)
    places = jnp.where(sends > 0, earlier, -1)
    return jnp.concatenate([places, jnp.sum(sends)[None]])


def peer_index(outer, side, core):
    return outer * 4 + side * 2 + core


def trip_pairs(section_total, outer_total, hop, cross, source_down, target_down):
    peers = 4 * outer_total
    pairs = []
    for section in range(1, section_total):
        for outer in range(outer_total):
            for side in range(2):
                for core in range(2):
                    source = (section - source_down) * peers + peer_index(outer, side, core)
                    target = peer_index((outer + hop) % outer_total, side ^ cross, core)
                    pairs.append((source, (section - target_down) * peers + target))
    return pairs


def after(value, *others):
    return lax.optimization_barrier((value,) + others)[0]


def exchange(blocks, stepped, places, peer_total, section_total, slots):
    outer_total = peer_total // 4
    partner = [(p, p ^ 1) for p in range(peer_total)]
    beyond = [(p, (p + 2 * (p % 2) - 1) % peer_total) for p in range(peer_total)]
    loads = load_ranges(outer_total)
    done = {}
    started = []
    for trip in expand(outer_total):
        name, hop, cross = trip
        pairs = functools.partial(trip_pairs, section_total, outer_total)
        if name in ("near", "far"):
            done[name] = lax.ppermute(stepped, "peer", partner if name == "near" else beyond)
            continue
        if name == "lift":
            block, pairs = blocks[name], pairs(0, 0, 0, 1)
        elif name == "swap":
            block, pairs = blocks[name], pairs(0, 1, 0, 0)
        elif name == "d":
            block, pairs = blocks[hop, cross], pairs(hop, cross, 0, 1)
        else:
            held = "lift" if name == "z" else "swap"
            first = 2 * loads[held].index((hop, cross))
            block = done[held][first : first + 2]
            pairs = pairs(hop, cross, 1, 1) if name == "z" else pairs(hop, 0, 0, 1)
        if len(started) == AHEAD - 1:
            block = after(block, done["near"])
        elif len(started) >= AHEAD:
            block = after(block, started[len(started) - AHEAD])
        held = name if name in ("lift", "swap") else (hop, cross)
        done[held] = lax.ppermute(block, AXES, pairs)
        started.append(done[held])
    trips = [(hop, cross) for name, hop, cross in expand(outer_total) if name in "dzr"]
    arrived = [done[trip] for trip in trips]
    crossing = jnp.concatenate([part[1:] for part in arrived])
    near, far = done["near"], done["far"]
    crossing, near, far, places = lax.optimization_barrier((crossing, near, far, places))
    crossed = lax.ppermute(crossing, "peer", partner)
    kept = [part[:1] for part in arrived]
    routed, averaged = place_kept(outer_total, trips, places, kept, (near, stepped, far), slots)
    routed = place_crossed(outer_total, trips, places, crossed, routed)
    return routed, averaged


def per_device(saved_inputs, incoming, norm_gain, adapter, wiring, counts):
    peer_total = lax.axis_size("peer")
    section_total = lax.axis_size("section")
    outer_total = peer_total // 4
    section, peer = lax.axis_index("section"), lax.axis_index("peer")
    slots = saved_inputs.shape[2]
    blocks, stepped = step(
        outer_total, saved_inputs[0, 0], incoming[0, 0], norm_gain[0], adapter[0, 0], wiring, counts
    )
    places = arrival_places(section, peer, section_total, wiring, counts)
    routed, averaged = exchange(blocks, stepped, places, peer_total, section_total, slots)
    return (routed[None, None], averaged[None, None])


def solution(mesh):
    return jax.shard_map(
        per_device,
        mesh=mesh,
        in_specs=(
            P("section", "peer", None, None, None),
            P("section", "peer", None, None, None),
            P("section", "peer", None),
            P("section", "peer", None, None, None),
            P(),
            P(),
        ),
        out_specs=(P("section", "peer", None, None, None), P("section", "peer", None, None, None)),
        check_vma=False,
    )
```
